32 devices in a mesh: parts: 2 (over y), row: 4 (over z), col: 2 (over x), cores: 2 (over core).
Axes of the slice: x: 2, y: 2, z: 4, core: 2. Of those that a mesh axis runs over, the one named last changes fastest.
Arguments:
- latent: float32 [128, 256, 128], P(('parts', 'row', 'cores'), 'col'), parts along dimension 0, may hold values from -6 to 6
- moment_one: float32 [128, 256, 128], P(('parts', 'row', 'cores'), 'col'), parts along dimension 0, may hold values from -0.3 to 0.3
- moment_two: float32 [128, 256, 128], P(('parts', 'row', 'cores'), 'col'), parts along dimension 0, may hold values from 0.001 to 0.01
- hole_mask: int32 [128, 256], P(('parts', 'row', 'cores'), 'col'), parts along dimension 0, may hold values 0 or 1
- target_rgb: float32 [3, 128, 256], P(None, ('parts', 'row', 'cores'), 'col'), parts along dimension 1, may hold values from -4 to 4
- kernel_one: bfloat16 [3, 3, 128, 128], replicated, may hold values from -0.1875 to 0.1875
- bias_one: float32 [128], replicated, may hold values from -3 to 3
- kernel_two: bfloat16 [3, 3, 128, 128], replicated, may hold values from -0.1875 to 0.1875
- bias_two: float32 [128], replicated, may hold values from -3 to 3
- rgb_weight: bfloat16 [3, 128], replicated, may hold values from -0.5 to 0.5
Outputs:
- latent_out: float32 [128, 256, 128], P(('parts', 'row', 'cores'), 'col'), parts along dimension 0
- moment_one_out: float32 [128, 256, 128], P(('parts', 'row', 'cores'), 'col'), parts along dimension 0
- moment_two_out: float32 [128, 256, 128], P(('parts', 'row', 'cores'), 'col'), parts along dimension 0
The draws below stay inside these ranges and needn't reach their ends.
There are 2 independent parts, one for each index of `parts`. The reference program is written for one: setup_inputs(seed, part) draws one part's arguments, and reference() takes and returns one part's arrays. A program takes and returns all parts, laid end to end along the dimension named above; an argument that names none is the same for every part. Nothing has to cross between parts.
All inputs are finite; a program needn't handle non-finite values. No bound on the sum of `hole_mask` on one device may be relied on, other than what follows from the above.
Results may differ from the reference program's by a relative error of at most 0.0045.
Values may be sent and summed in bfloat16 or wider, within the bound.
A program may use at most 64 MiB of HBM per device.

```python
import math
import jax
import jax.numpy as jnp
from jax import lax

C = 128
STEPS = 2
H = 64
W = 256


def touch_ends(array, key, least, largest):
    longest = array.shape.index(max(array.shape))
    spots = []
    for shift in (0, 1):
        where = [jax.random.randint(jax.random.fold_in(key, axis), (), 0, length) for axis, length in enumerate(array.shape)]
        where[longest] = (where[longest] + shift) % array.shape[longest]
        spots.append(tuple(where))
    return array.at[spots[0]].set(least).at[spots[1]].set(largest)


def shard_levels(rng, extent, cuts, least, top_value):
    factor_of, own = 1.0, jax.random.fold_in(rng, 6)
    for position, shards_of in cuts:
        heights = jnp.exp(jax.random.uniform(jax.random.fold_in(own, position), (shards_of,), jnp.float32, least / len(cuts), top_value / len(cuts)))
        factor_of = factor_of * jnp.repeat(heights, extent[position] // shards_of).reshape([-1 if axis == position else 1 for axis in range(len(extent))])
    return factor_of


def noise(key, shape, width, limit, split=(), kind=jnp.bfloat16):
    values = width * jax.random.normal(key, shape, jnp.float32)
    if split:
        values = values * shard_levels(key, shape, split, -0.22, 0.18)
    return jnp.clip(values, -limit, limit).astype(kind)


def setup_inputs(seed: int = 0, part: int = 0) -> dict:
    key_list = jax.random.split(jax.random.key(seed), 11)
    own_keys = jax.random.split(jax.random.fold_in(key_list[10], part), 11)
    return {
        "latent": noise(own_keys[0], (H, W, C), 1.0, 6.0, ((0, 8), (1, 2)), jnp.float32),
        "moment_one": noise(own_keys[1], (H, W, C), 0.05, 0.3, ((0, 8), (1, 2)), jnp.float32),
        "moment_two": jnp.clip(jnp.exp(math.log(0.01) - 2.30258502 * jax.random.uniform(own_keys[2], (H, W, C), jnp.float32) ** shard_levels(own_keys[2], (H, W, C), ((0, 8), (1, 2)), -0.2, 0.2)), 0.001, 0.01),
        "hole_mask": touch_ends((jax.random.randint(own_keys[3], (H, W), 0, 2) < 1).astype(jnp.int32), jax.random.fold_in(own_keys[3], 1), 0, 1),
        "target_rgb": noise(own_keys[4], (3, H, W), 1.0, 4.0, ((1, 8), (2, 2)), jnp.float32),
        "kernel_one": noise(key_list[5], (3, 3, C, C), (9 * C) ** -0.5, 0.1875),
        "bias_one": noise(key_list[6], (C,), 0.5, 3.0, (), jnp.float32),
        "kernel_two": noise(key_list[7], (3, 3, C, C), (9 * C) ** -0.5, 0.1875),
        "bias_two": noise(key_list[8], (C,), 0.5, 3.0, (), jnp.float32),
        "rgb_weight": noise(key_list[9], (3, C), C ** -0.5, 0.5),
    }


BETA_ONE = 0.6
BETA_TWO = 0.9
LEARN_RATE = 0.4
EPSILON = 1e-08

def convolve(padded, kernel, height, breadth, transposed):
    channels = padded.shape[2]
    weights = kernel.astype(jnp.float32)
    summed = None
    for tap_row in range(3):
        for tap_col in range(3):
            if transposed:
                section = padded[2 - tap_row:2 - tap_row + height, 2 - tap_col:2 - tap_col + breadth]
                matrix = weights[tap_row, tap_col].T
            else:
                section = padded[tap_row:tap_row + height, tap_col:tap_col + breadth]
                matrix = weights[tap_row, tap_col]
            product = jnp.dot(section.reshape(height * breadth, channels).astype(jnp.float32), matrix, precision=lax.Precision.HIGHEST, preferred_element_type=jnp.float32)
            summed = product if summed is None else summed + product
    return summed.reshape(height, breadth, -1)

def padding(field):
    return jnp.pad(field, ((1, 1), (1, 1), (0, 0)))

def silu_slope(value):
    sigma = jax.nn.sigmoid(value)
    return sigma * (1.0 + value * (1.0 - sigma))

def reference(latent, moment_one, moment_two, hole_mask, target_rgb, kernel_one, bias_one, kernel_two, bias_two, rgb_weight):
    height, breadth = (latent.shape[0], latent.shape[1])
    current, first, second = (latent, moment_one, moment_two)
    known = hole_mask.astype(jnp.float32)
    projection = rgb_weight.astype(jnp.float32)
    for iteration in range(STEPS):
        rounded = current.astype(jnp.bfloat16)
        pre_one = convolve(padding(rounded), kernel_one, height, breadth, False) + bias_one
        hidden_one = jax.nn.silu(pre_one).astype(jnp.bfloat16)
        pre_two = convolve(padding(hidden_one), kernel_two, height, breadth, False) + bias_two
        hidden_two = jax.nn.silu(pre_two).astype(jnp.bfloat16)
        color = jnp.einsum('yxc,kc->kyx', hidden_two.astype(jnp.float32), projection, precision=lax.Precision.HIGHEST)
        residual = known[None] * (color - target_rgb)
        grad_hidden = jnp.einsum('kyx,kc->yxc', residual, projection, precision=lax.Precision.HIGHEST)
        grad_two = (grad_hidden * silu_slope(pre_two)).astype(jnp.bfloat16)
        grad_inner = convolve(padding(grad_two), kernel_two, height, breadth, True)
        grad_one = (grad_inner * silu_slope(pre_one)).astype(jnp.bfloat16)
        gradient = convolve(padding(grad_one), kernel_one, height, breadth, True)
        first = BETA_ONE * first + (1.0 - BETA_ONE) * gradient
        second = BETA_TWO * second + (1.0 - BETA_TWO) * gradient * gradient
        current = current - LEARN_RATE * first / (jnp.sqrt(second) + EPSILON)
    return (current, first, second)
```

```python
import functools

import jax
import jax.numpy as jnp
from jax import lax
from jax.experimental import pallas as pl
from jax.experimental.pallas import tpu as pltpu
from jax.sharding import PartitionSpec as P

STEPS = 2
BETA_ONE = 0.6
BETA_TWO = 0.9
LEARN_RATE = 0.4
EPSILON = 1e-08

MESH = pl.DeviceIdType.MESH
HALO = 4
WRAP = 16
DIRS = [(-1, 0), (1, 0), (0, -1), (0, 1), (-1, -1), (-1, 1), (1, -1), (1, 1)]
UNROLL = False


def sweep(fn, low, high):
    if UNROLL:
        for q in range(low, high):
            fn(q)
    elif high > low:

        def turn(q, carry):
            fn(q)
            return carry

        lax.fori_loop(low, high, turn, 0)


def kernel(
    height,
    breadth,
    rows_n,
    cols_n,
    cores_n,
    latent_hbm,
    one_hbm,
    two_hbm,
    mask_hbm,
    target_hbm,
    kone_hbm,
    ktwo_hbm,
    bone_ref,
    btwo_ref,
    rgb_ref,
    latent_out,
    one_out,
    two_out,
    z_ref,
    m_ref,
    v_ref,
    maski,
    aux,
    aux_in,
    stage,
    row_in,
    col_in,
    diag_in,
    zx,
    h1,
    g2,
    g1,
    slope1,
    weights,
    wide,
    rgb_f,
    rgb_t,
    rgb_b,
    target_p,
    target_t,
    mask_t,
    local_sem,
    out_sem,
    send_sem,
    recv_sem,
    aux_send,
    aux_recv,
):
    width = breadth + WRAP
    place = lax.axis_index("row") * cores_n + lax.axis_index("cores")
    col = lax.axis_index("col")
    ranks = rows_n * cores_n

    def there(d):
        dr, dc = d
        ok = None
        if dr:
            ok = place > 0 if dr < 0 else place < ranks - 1
        if dc:
            side = col > 0 if dc < 0 else col < cols_n - 1
            ok = side if ok is None else jnp.logical_and(ok, side)
        return ok

    def peer(d):
        spot = place + d[0]
        return {
            "row": spot // cores_n,
            "cores": lax.rem(spot, cores_n),
            "col": col + d[1],
        }

    live = [d for d in DIRS if not (d[1] and cols_n == 1) and not (d[0] and ranks == 1)]
    slot = {d: i for i, d in enumerate(DIRS)}

    def back(d):
        return (-d[0], -d[1])

    def local(src, dst, i):
        return pltpu.make_async_copy(src, dst, local_sem.at[i])

    loads = [
        local(latent_hbm, z_ref, 0),
        local(target_hbm, aux.at[pl.ds(0, 3)], 1),
        local(mask_hbm, maski, 2),
        local(ktwo_hbm, weights.at[1, pl.ds(0, 9 * 128), pl.ds(0, 128)], 3),
        local(kone_hbm, weights.at[0, pl.ds(0, 9 * 128), pl.ds(0, 128)], 4),
        local(kone_hbm, weights.at[0, pl.ds(384, 9 * 128), pl.ds(128, 128)], 5),
        local(ktwo_hbm, weights.at[1, pl.ds(384, 9 * 128), pl.ds(128, 128)], 6),
        local(one_hbm, m_ref, 7),
        local(two_hbm, v_ref, 8),
    ]
    for c in loads:
        c.start()

    barrier = pltpu.get_barrier_semaphore()
    for d in live:

        @pl.when(there(d))
        def _():
            pl.semaphore_signal(barrier, inc=1, device_id=peer(d), device_id_type=MESH)

    def landing(d, step):
        if d[1] == 0:
            return row_in.at[step, 0 if d[0] < 0 else 1]
        if d[0] == 0:
            return col_in.at[step, 0 if d[1] < 0 else 1]
        return diag_in.at[step, 0 if d[0] < 0 else 1, 0 if d[1] < 0 else 1]

    def outgoing(d, step):
        rows = {0: pl.ds(0, height), -1: pl.ds(0, HALO), 1: pl.ds(height - HALO, HALO)}[d[0]]
        cols = {0: pl.ds(0, breadth), -1: pl.ds(0, WRAP), 1: pl.ds(breadth - WRAP, WRAP)}[d[1]]
        return stage.at[step, rows, cols]

    def halo_copy(d, step):
        return pltpu.make_async_remote_copy(
            src_ref=outgoing(d, step),
            dst_ref=landing(back(d), step),
            send_sem=send_sem.at[step, slot[d]],
            recv_sem=recv_sem.at[step, slot[back(d)]],
            device_id=peer(d),
            device_id_type=MESH,
        )

    def halo_arrival(d, step):
        return pltpu.make_async_remote_copy(
            src_ref=outgoing(back(d), step),
            dst_ref=landing(d, step),
            send_sem=send_sem.at[step, slot[back(d)]],
            recv_sem=recv_sem.at[step, slot[d]],
            device_id=peer(d),
            device_id_type=MESH,
        )

    def aux_copy(d):
        return pltpu.make_async_remote_copy(
            src_ref=aux,
            dst_ref=aux_in.at[slot[back(d)]],
            send_sem=aux_send.at[slot[d]],
            recv_sem=aux_recv.at[slot[back(d)]],
            device_id=peer(d),
            device_id_type=MESH,
        )

    def aux_arrival(d):
        return pltpu.make_async_remote_copy(
            src_ref=aux,
            dst_ref=aux_in.at[slot[d]],
            send_sem=aux_send.at[slot[back(d)]],
            recv_sem=aux_recv.at[slot[d]],
            device_id=peer(d),
            device_id_type=MESH,
        )

    def for_each(dirs, fn):
        for d in dirs:
            if d in live:

                @pl.when(there(d))
                def _():
                    fn(d)

    def clear(d):
        for step in range(STEPS):
            ref = landing(d, step)
            ref[...] = jnp.zeros(ref.shape, ref.dtype)
        aux_in[slot[d]] = jnp.zeros(aux_in.shape[1:], aux_in.dtype)

    for d in DIRS:
        if d not in live:
            clear(d)
        else:

            @pl.when(jnp.logical_not(there(d)))
            def _():
                clear(d)

    sides = [d for d in DIRS if d[0] == 0]
    verticals = [d for d in DIRS if d[0] != 0]
    uppers = [d for d in DIRS if d[0] < 0]
    lowers = [d for d in DIRS if d[0] > 0]

    loads[0].wait()
    stage[0] = z_ref[...].astype(jnp.bfloat16)
    peers = jnp.int32(0)
    for d in live:
        peers = peers + there(d).astype(jnp.int32)
    pl.semaphore_wait(barrier, peers)

    for_each(verticals + sides, lambda d: halo_copy(d, 0).start())
    loads[1].wait()
    loads[2].wait()
    aux[3] = maski[...].astype(jnp.float32)
    for_each(DIRS, lambda d: aux_copy(d).start())

    zero_block = jnp.zeros((384, 128), jnp.bfloat16)
    for i in range(4):
        weights[i, pl.ds(9 * 128, 384), pl.ds(0, 128)] = zero_block
        weights[i, pl.ds(0, 384), pl.ds(128, 128)] = zero_block
    for i in range(3, 7):
        loads[i].wait()

    def turned(layer):
        def flip(tap, carry):
            block = weights[layer, pl.ds(pl.multiple_of(tap * 128, 128), 128), pl.ds(0, 128)]
            block = block.astype(jnp.float32).T.astype(jnp.bfloat16)
            spot = pl.multiple_of((8 - tap) * 128, 128)
            weights[2 + layer, pl.ds(spot, 128), pl.ds(0, 128)] = block
            weights[2 + layer, pl.ds(pl.multiple_of(spot + 384, 128), 128), pl.ds(128, 128)] = block
            return carry

        lax.fori_loop(0, 9, flip, 0)

    turned(1)
    turned(0)

    rgb_f[...] = jnp.zeros(rgb_f.shape, jnp.float32)
    projection = rgb_ref[...].astype(jnp.float32)
    rgb_f[pl.ds(0, 3), pl.ds(0, 128)] = projection
    rgb_f[pl.ds(3, 3), pl.ds(128, 128)] = projection
    full = rgb_f[...]
    rgb_t[...] = full.T.astype(jnp.bfloat16)
    rgb_b[pl.ds(0, 128)] = full.astype(jnp.bfloat16)
    rgb_b[pl.ds(128, 128)] = full.astype(jnp.bfloat16)

    spots = lax.broadcasted_iota(jnp.int32, (width, 256), 0)
    right_ok = (col < cols_n - 1).astype(jnp.float32)
    left_ok = (col > 0).astype(jnp.float32)
    wide[...] = jnp.where(
        spots < breadth, 1.0, jnp.where(spots < breadth + WRAP // 2, right_ok, left_ok)
    )
    up_ok = (place > 0).astype(jnp.float32)
    down_ok = (place < ranks - 1).astype(jnp.float32)

    def row_ok(row):
        return jnp.where(row < 0, up_ok, jnp.where(row >= height, down_ok, 1.0))

    lane_half = lax.broadcasted_iota(jnp.int32, (1, 256), 1) < 128

    for_each(DIRS, lambda d: aux_arrival(d).wait_recv())
    target_p[...] = jnp.zeros(target_p.shape, jnp.float32)
    target_t[...] = jnp.zeros(target_t.shape, jnp.float32)
    mask_t[...] = jnp.zeros(mask_t.shape, jnp.float32)
    pairs_two = (height + 4) // 2
    near = lax.broadcasted_iota(jnp.int32, (4, 128), 1) < WRAP // 2
    for r in range(-2, height + 2):
        if r < 0:
            mid, left, right, at = ((-1, 0), (-1, -1), (-1, 1), height + r)
        elif r < height:
            mid, left, right, at = (None, (0, -1), (0, 1), r)
        else:
            mid, left, right, at = ((1, 0), (1, -1), (1, 1), r - height)
        center = aux[:, at, :] if mid is None else aux_in[slot[mid], :, at, :]
        from_left = aux_in[slot[left], :, at, pl.ds(breadth - 128, 128)]
        from_right = aux_in[slot[right], :, at, pl.ds(0, 128)]
        tail = jnp.where(near, from_right, pltpu.roll(from_left, WRAP, 1))
        q, half = divmod(r + 2, 2)
        for part, lanes in ((center, pl.ds(0, breadth)), (tail, pl.ds(breadth, 128))):
            target_p[q, pl.ds(3 * half, 3), lanes] = part[0:3]
            for k in range(3):
                target_p[q, pl.ds(8 + 3 * half + k, 1), lanes] = part[3:4]
    for q in range(pairs_two):
        target_t[q, :, pl.ds(0, 8)] = target_p[q, pl.ds(0, 8)].T[0:width]
        mask_t[q, :, pl.ds(0, 8)] = target_p[q, pl.ds(8, 8)].T[0:width]

    bias_one = jnp.concatenate([bone_ref[...], bone_ref[...]], axis=1)
    bias_two = jnp.concatenate([btwo_ref[...], btwo_ref[...]], axis=1)

    def put(ref, row, value):
        ref[row, :, pl.ds(0, 128)] = pltpu.roll(value, 1, 0).astype(jnp.bfloat16)
        ref[row, :, pl.ds(128, 128)] = value.astype(jnp.bfloat16)
        ref[row, :, pl.ds(256, 128)] = pltpu.roll(value, width - 1, 0).astype(jnp.bfloat16)

    def put_pair(ref, q, value):
        put(ref, 2 * q, value[:, 0:128])
        put(ref, 2 * q + 1, value[:, 128:256])

    def conv(ref, q, which, count):
        window = jnp.concatenate(
            [ref[2 * q + i, pl.ds(0, count), :] for i in range(4)], axis=1
        )
        return jnp.dot(window, weights[which], preferred_element_type=jnp.float32)

    def parts_of(pre):
        turn = 0.5 * jnp.tanh(0.5 * pre)
        return 0.5 + turn, 0.5 - turn

    tail_pick = lax.broadcasted_iota(jnp.int32, (WRAP, 128), 0) < WRAP // 2

    def expand(row, middle, from_left, from_right):
        tail = jnp.where(
            tail_pick, from_right.astype(jnp.float32), from_left.astype(jnp.float32)
        )
        put(zx, row, jnp.concatenate([middle.astype(jnp.float32), tail], axis=0))

    def first_layer(q):
        pre = conv(zx, q, 0, width) + bias_one
        sigma, rest = parts_of(pre)
        row = 2 * q - 3
        inside = jnp.where(lane_half, row_ok(row), row_ok(row + 1))
        kept = sigma * (wide[...] * inside)
        hidden = pre * kept
        slope1[q] = kept + hidden * rest
        put_pair(h1, q, hidden)

    def second_layer(q):
        pre = conv(h1, q, 1, width) + bias_two
        sigma, rest = parts_of(pre)
        hidden = pre * sigma
        slope = sigma + hidden * rest
        color = jnp.dot(
            hidden.astype(jnp.bfloat16), rgb_t[...], preferred_element_type=jnp.float32
        )
        residual = mask_t[q] * (color - target_t[q])
        coarse = residual.astype(jnp.bfloat16)
        fine = (residual - coarse.astype(jnp.float32)).astype(jnp.bfloat16)
        grad = jnp.dot(
            jnp.concatenate([coarse, fine], axis=1),
            rgb_b[...],
            preferred_element_type=jnp.float32,
        )
        put_pair(g2, q, grad * slope)

    def back_second(q):
        put_pair(g1, q, conv(g2, q, 3, width) * slope1[q + 1])

    half = height // 2
    cuts = (
        (first_layer, 2, 1 + half, half + 3),
        (second_layer, 2, half, half + 2),
        (back_second, 2, max(2, half - 1), half + 1),
    )

    for step in range(STEPS):
        last = step == STEPS - 1
        for_each(sides, lambda d: halo_arrival(d, step).wait_recv())

        def own_row(r):
            expand(
                r + HALO, stage[step, r], col_in[step, 0, r], col_in[step, 1, r]
            )

        sweep(own_row, 0, height)
        for fn, low, high, _ in cuts:
            sweep(fn, low, high)
        for_each(verticals, lambda d: halo_arrival(d, step).wait_recv())

        def halo_row(r):
            expand(r, row_in[step, 0, r], diag_in[step, 0, 0, r], diag_in[step, 0, 1, r])
            expand(
                r + HALO + height,
                row_in[step, 1, r],
                diag_in[step, 1, 0, r],
                diag_in[step, 1, 1, r],
            )

        sweep(halo_row, 0, HALO)
        for fn, low, high, count in cuts:
            sweep(fn, 0, low)
            sweep(fn, high, count)

        if step == 0:
            loads[7].wait()
            loads[8].wait()

        for q in range(half):
            grads = conv(g1, q, 2, breadth)
            for i in range(2):
                r = 2 * q + i
                grad = grads[:, 128 * i : 128 * (i + 1)]
                first = BETA_ONE * m_ref[r] + (1.0 - BETA_ONE) * grad
                second = BETA_TWO * v_ref[r] + (1.0 - BETA_TWO) * grad * grad
                fresh = z_ref[r] - LEARN_RATE * first / (jnp.sqrt(second) + EPSILON)
                m_ref[r] = first
                v_ref[r] = second
                z_ref[r] = fresh
                if not last:
                    stage[step + 1, r] = fresh.astype(jnp.bfloat16)
            if last:
                for i, (src, dst) in enumerate(
                    ((z_ref, latent_out), (m_ref, one_out), (v_ref, two_out))
                ):
                    rows = pl.ds(2 * q, 2)
                    pltpu.make_async_copy(
                        src.at[rows], dst.at[rows], out_sem.at[i, q]
                    ).start()
            elif 2 * (q + 1) == HALO:
                for_each(uppers, lambda d: halo_copy(d, step + 1).start())
        if not last:
            for_each(lowers + sides, lambda d: halo_copy(d, step + 1).start())

    for step in range(STEPS):
        for_each(DIRS, lambda d: halo_copy(d, step).wait_send())
    for_each(DIRS, lambda d: aux_copy(d).wait_send())
    for q in range(half):
        for i, (src, dst) in enumerate(((z_ref, latent_out), (m_ref, one_out), (v_ref, two_out))):
            rows = pl.ds(2 * q, 2)
            pltpu.make_async_copy(src.at[rows], dst.at[rows], out_sem.at[i, q]).wait()


def body(
    sizes,
    latent,
    moment_one,
    moment_two,
    hole_mask,
    target_rgb,
    kernel_one,
    bias_one,
    kernel_two,
    bias_two,
    rgb_weight,
):
    height, breadth, channels = latent.shape
    width = breadth + WRAP
    rows_n, cols_n, cores_n = sizes
    f32, bf16 = jnp.float32, jnp.bfloat16
    anywhere = pl.BlockSpec(memory_space=pl.ANY)
    near = pl.BlockSpec(memory_space=pltpu.VMEM)
    tile = jax.ShapeDtypeStruct(latent.shape, f32)
    half = height // 2
    scratch = [
        pltpu.VMEM((height, breadth, channels), f32),
        pltpu.VMEM((height, breadth, channels), f32),
        pltpu.VMEM((height, breadth, channels), f32),
        pltpu.VMEM((height, breadth), jnp.int32),
        pltpu.VMEM((4, height, breadth), f32),
        pltpu.VMEM((8, 4, height, breadth), f32),
        pltpu.VMEM((STEPS, height, breadth, channels), bf16),
        pltpu.VMEM((STEPS, 2, HALO, breadth, channels), bf16),
        pltpu.VMEM((STEPS, 2, height, WRAP, channels), bf16),
        pltpu.VMEM((STEPS, 2, 2, HALO, WRAP, channels), bf16),
        pltpu.VMEM((height + 8, width, 3 * channels), bf16),
        pltpu.VMEM((height + 6, width, 3 * channels), bf16),
        pltpu.VMEM((height + 4, width, 3 * channels), bf16),
        pltpu.VMEM((height + 2, width, 3 * channels), bf16),
        pltpu.VMEM((half + 3, width, 2 * channels), f32),
        pltpu.VMEM((4, 12 * channels, 2 * channels), bf16),
        pltpu.VMEM((width, 2 * channels), f32),
        pltpu.VMEM((128, 2 * channels), f32),
        pltpu.VMEM((2 * channels, 128), bf16),
        pltpu.VMEM((256, 2 * channels), bf16),
        pltpu.VMEM((half + 2, 16, breadth + 128), f32),
        pltpu.VMEM((half + 2, width, 128), f32),
        pltpu.VMEM((half + 2, width, 128), f32),
        pltpu.SemaphoreType.DMA((9,)),
        pltpu.SemaphoreType.DMA((3, half)),
        pltpu.SemaphoreType.DMA((STEPS, 8)),
        pltpu.SemaphoreType.DMA((STEPS, 8)),
        pltpu.SemaphoreType.DMA((8,)),
        pltpu.SemaphoreType.DMA((8,)),
    ]
    return pl.pallas_call(
        functools.partial(kernel, height, breadth, rows_n, cols_n, cores_n),
        out_shape=(tile, tile, tile),
        in_specs=[anywhere] * 7 + [near] * 3,
        out_specs=(anywhere, anywhere, anywhere),
        scratch_shapes=scratch,
        compiler_params=pltpu.CompilerParams(
            collective_id=0, has_side_effects=True, vmem_limit_bytes=48 * 1024 * 1024
        ),
        name="inpaint",
    )(
        latent,
        moment_one,
        moment_two,
        hole_mask,
        target_rgb,
        kernel_one.reshape(9 * channels, channels),
        kernel_two.reshape(9 * channels, channels),
        bias_one.reshape(1, channels),
        bias_two.reshape(1, channels),
        rgb_weight,
    )


def solution(mesh):
    sizes = (mesh.shape["row"], mesh.shape["col"], mesh.shape["cores"])
    tile = P(("parts", "row", "cores"), "col", None)
    return jax.shard_map(
        functools.partial(body, sizes),
        mesh=mesh,
        in_specs=(
            tile,
            tile,
            tile,
            P(("parts", "row", "cores"), "col"),
            P(None, ("parts", "row", "cores"), "col"),
            P(),
            P(),
            P(),
            P(),
            P(),
        ),
        out_specs=(tile, tile, tile),
        check_vma=False,
    )
```

```python
import functools

import jax
import jax.numpy as jnp
from jax import lax
from jax.experimental import pallas as pl
from jax.experimental.pallas import tpu as pltpu
from jax.sharding import PartitionSpec as P

STEPS = 2
BETA_ONE = 0.6
BETA_TWO = 0.9
LEARN_RATE = 0.4
EPSILON = 1e-08

MESH = pl.DeviceIdType.MESH
HALO = 4
WRAP = 16
DIRS = [(-1, 0), (1, 0), (0, -1), (0, 1), (-1, -1), (-1, 1), (1, -1), (1, 1)]


def sweep(product, finish, places):
    ready = product(places[0])
    for at, q in enumerate(places):
        held = ready
        if at + 1 < len(places):
            ready = product(places[at + 1])
        finish(q, held)


def kernel(
    height,
    breadth,
    rows_n,
    cols_n,
    cores_n,
    latent_hbm,
    one_hbm,
    two_hbm,
    mask_hbm,
    target_hbm,
    kone_hbm,
    ktwo_hbm,
    bone_ref,
    btwo_ref,
    rgb_ref,
    latent_out,
    one_out,
    two_out,
    grad_out,
    z_ref,
    m_ref,
    v_ref,
    grad_ref,
    maski,
    aux,
    aux_in,
    stage,
    row_in,
    col_in,
    diag_in,
    zx,
    h1,
    g2,
    g1,
    slope1,
    weights,
    wide,
    rgb_f,
    rgb_t,
    rgb_b,
    target_p,
    target_t,
    mask_t,
    local_sem,
    out_sem,
    send_sem,
    recv_sem,
    aux_send,
    aux_recv,
):
    width = breadth + WRAP
    place = lax.axis_index("row") * cores_n + lax.axis_index("cores")
    col = lax.axis_index("col")
    ranks = rows_n * cores_n

    def there(d):
        dr, dc = d
        ok = None
        if dr:
            ok = place > 0 if dr < 0 else place < ranks - 1
        if dc:
            side = col > 0 if dc < 0 else col < cols_n - 1
            ok = side if ok is None else jnp.logical_and(ok, side)
        return ok

    def peer(d):
        spot = place + d[0]
        return {
            "row": spot // cores_n,
            "cores": lax.rem(spot, cores_n),
            "col": col + d[1],
        }

    live = [d for d in DIRS if not (d[1] and cols_n == 1) and not (d[0] and ranks == 1)]
    slot = {d: i for i, d in enumerate(DIRS)}

    def back(d):
        return (-d[0], -d[1])

    def local(src, dst, i):
        return pltpu.make_async_copy(src, dst, local_sem.at[i])

    loads = [
        local(latent_hbm, z_ref, 0),
        local(target_hbm, aux.at[pl.ds(0, 3)], 1),
        local(mask_hbm, maski, 2),
        local(ktwo_hbm, weights.at[1, pl.ds(0, 9 * 128), pl.ds(0, 128)], 3),
        local(kone_hbm, weights.at[0, pl.ds(0, 9 * 128), pl.ds(0, 128)], 4),
        local(kone_hbm, weights.at[0, pl.ds(384, 9 * 128), pl.ds(128, 128)], 5),
        local(ktwo_hbm, weights.at[1, pl.ds(384, 9 * 128), pl.ds(128, 128)], 6),
        local(one_hbm, m_ref, 7),
        local(two_hbm, v_ref, 8),
    ]
    for c in loads:
        c.start()

    barrier = pltpu.get_barrier_semaphore()
    for d in live:

        @pl.when(there(d))
        def _():
            pl.semaphore_signal(barrier, inc=1, device_id=peer(d), device_id_type=MESH)

    def landing(d, step):
        if d[1] == 0:
            return row_in.at[step, 0 if d[0] < 0 else 1]
        if d[0] == 0:
            return col_in.at[step, 0 if d[1] < 0 else 1]
        return diag_in.at[step, 0 if d[0] < 0 else 1, 0 if d[1] < 0 else 1]

    def outgoing(d, step):
        rows = {0: pl.ds(0, height), -1: pl.ds(0, HALO), 1: pl.ds(height - HALO, HALO)}[d[0]]
        cols = {0: pl.ds(0, breadth), -1: pl.ds(0, WRAP), 1: pl.ds(breadth - WRAP, WRAP)}[d[1]]
        return stage.at[step, rows, cols]

    def halo_copy(d, step):
        return pltpu.make_async_remote_copy(
            src_ref=outgoing(d, step),
            dst_ref=landing(back(d), step),
            send_sem=send_sem.at[step, slot[d]],
            recv_sem=recv_sem.at[step, slot[back(d)]],
            device_id=peer(d),
            device_id_type=MESH,
        )

    def halo_arrival(d, step):
        return pltpu.make_async_remote_copy(
            src_ref=outgoing(back(d), step),
            dst_ref=landing(d, step),
            send_sem=send_sem.at[step, slot[back(d)]],
            recv_sem=recv_sem.at[step, slot[d]],
            device_id=peer(d),
            device_id_type=MESH,
        )

    def aux_copy(d):
        return pltpu.make_async_remote_copy(
            src_ref=aux,
            dst_ref=aux_in.at[slot[back(d)]],
            send_sem=aux_send.at[slot[d]],
            recv_sem=aux_recv.at[slot[back(d)]],
            device_id=peer(d),
            device_id_type=MESH,
        )

    def aux_arrival(d):
        return pltpu.make_async_remote_copy(
            src_ref=aux,
            dst_ref=aux_in.at[slot[d]],
            send_sem=aux_send.at[slot[back(d)]],
            recv_sem=aux_recv.at[slot[d]],
            device_id=peer(d),
            device_id_type=MESH,
        )

    def for_each(dirs, fn):
        for d in dirs:
            if d in live:

                @pl.when(there(d))
                def _():
                    fn(d)

    def clear(d):
        for step in range(STEPS):
            ref = landing(d, step)
            ref[...] = jnp.zeros(ref.shape, ref.dtype)
        aux_in[slot[d]] = jnp.zeros(aux_in.shape[1:], aux_in.dtype)

    for d in DIRS:
        if d not in live:
            clear(d)
        else:

            @pl.when(jnp.logical_not(there(d)))
            def _():
                clear(d)

    sides = [d for d in DIRS if d[0] == 0]
    verticals = [d for d in DIRS if d[0] != 0]
    uppers = [d for d in DIRS if d[0] < 0]
    lowers = [d for d in DIRS if d[0] > 0]

    loads[0].wait()
    stage[0] = z_ref[...].astype(jnp.bfloat16)
    peers = jnp.int32(0)
    for d in live:
        peers = peers + there(d).astype(jnp.int32)
    pl.semaphore_wait(barrier, peers)

    for_each(verticals + sides, lambda d: halo_copy(d, 0).start())
    loads[1].wait()
    loads[2].wait()
    aux[3] = maski[...].astype(jnp.float32)
    for_each(DIRS, lambda d: aux_copy(d).start())

    zero_block = jnp.zeros((384, 128), jnp.bfloat16)
    for i in range(4):
        weights[i, pl.ds(9 * 128, 384), pl.ds(0, 128)] = zero_block
        weights[i, pl.ds(0, 384), pl.ds(128, 128)] = zero_block
    for i in range(3, 7):
        loads[i].wait()

    def turned(layer):
        def flip(tap, carry):
            block = weights[layer, pl.ds(pl.multiple_of(tap * 128, 128), 128), pl.ds(0, 128)]
            block = block.astype(jnp.float32).T.astype(jnp.bfloat16)
            spot = pl.multiple_of((8 - tap) * 128, 128)
            weights[2 + layer, pl.ds(spot, 128), pl.ds(0, 128)] = block
            weights[2 + layer, pl.ds(pl.multiple_of(spot + 384, 128), 128), pl.ds(128, 128)] = block
            return carry

        lax.fori_loop(0, 9, flip, 0)

    turned(1)
    turned(0)

    rgb_f[...] = jnp.zeros(rgb_f.shape, jnp.float32)
    projection = rgb_ref[...].astype(jnp.float32)
    rgb_f[pl.ds(0, 3), pl.ds(0, 128)] = projection
    rgb_f[pl.ds(3, 3), pl.ds(128, 128)] = projection
    full = rgb_f[...]
    rgb_t[...] = full.T.astype(jnp.bfloat16)
    rgb_b[pl.ds(0, 128)] = full.astype(jnp.bfloat16)
    rgb_b[pl.ds(128, 128)] = full.astype(jnp.bfloat16)

    spots = lax.broadcasted_iota(jnp.int32, (width, 256), 0)
    right_ok = (col < cols_n - 1).astype(jnp.float32)
    left_ok = (col > 0).astype(jnp.float32)
    wide[...] = jnp.where(
        spots < breadth, 1.0, jnp.where(spots < breadth + WRAP // 2, right_ok, left_ok)
    )
    up_ok = (place > 0).astype(jnp.float32)
    down_ok = (place < ranks - 1).astype(jnp.float32)

    def row_ok(row):
        return jnp.where(row < 0, up_ok, jnp.where(row >= height, down_ok, 1.0))

    lane_half = lax.broadcasted_iota(jnp.int32, (1, 256), 1) < 128

    for_each(DIRS, lambda d: aux_arrival(d).wait_recv())
    target_p[...] = jnp.zeros(target_p.shape, jnp.float32)
    target_t[...] = jnp.zeros(target_t.shape, jnp.float32)
    mask_t[...] = jnp.zeros(mask_t.shape, jnp.float32)
    pairs_two = (height + 4) // 2
    near = lax.broadcasted_iota(jnp.int32, (4, 128), 1) < WRAP // 2
    for r in range(-2, height + 2):
        if r < 0:
            mid, left, right, at = ((-1, 0), (-1, -1), (-1, 1), height + r)
        elif r < height:
            mid, left, right, at = (None, (0, -1), (0, 1), r)
        else:
            mid, left, right, at = ((1, 0), (1, -1), (1, 1), r - height)
        center = aux[:, at, :] if mid is None else aux_in[slot[mid], :, at, :]
        from_left = aux_in[slot[left], :, at, pl.ds(breadth - 128, 128)]
        from_right = aux_in[slot[right], :, at, pl.ds(0, 128)]
        tail = jnp.where(near, from_right, pltpu.roll(from_left, WRAP, 1))
        q, half = divmod(r + 2, 2)
        for part, lanes in ((center, pl.ds(0, breadth)), (tail, pl.ds(breadth, 128))):
            target_p[q, pl.ds(3 * half, 3), lanes] = part[0:3]
            for k in range(3):
                target_p[q, pl.ds(8 + 3 * half + k, 1), lanes] = part[3:4]
    for q in range(pairs_two):
        target_t[q, :, pl.ds(0, 8)] = target_p[q, pl.ds(0, 8)].T[0:width]
        mask_t[q, :, pl.ds(0, 8)] = target_p[q, pl.ds(8, 8)].T[0:width]

    bias_one = jnp.concatenate([bone_ref[...], bone_ref[...]], axis=1)
    bias_two = jnp.concatenate([btwo_ref[...], btwo_ref[...]], axis=1)

    def put(ref, row, value):
        ref[row, :, pl.ds(0, 128)] = pltpu.roll(value, 1, 0).astype(jnp.bfloat16)
        ref[row, :, pl.ds(128, 128)] = value.astype(jnp.bfloat16)
        ref[row, :, pl.ds(256, 128)] = pltpu.roll(value, width - 1, 0).astype(jnp.bfloat16)

    def put_pair(ref, q, value):
        put(ref, 2 * q, value[:, 0:128])
        put(ref, 2 * q + 1, value[:, 128:256])

    def conv(ref, q, which, count):
        window = jnp.concatenate(
            [ref[2 * q + i, pl.ds(0, count), :] for i in range(4)], axis=1
        )
        return jnp.dot(window, weights[which], preferred_element_type=jnp.float32)

    def parts_of(pre):
        turn = 0.5 * jnp.tanh(0.5 * pre)
        return 0.5 + turn, 0.5 - turn

    tail_pick = lax.broadcasted_iota(jnp.int32, (WRAP, 128), 0) < WRAP // 2

    def expand(row, middle, from_left, from_right):
        tail = jnp.where(
            tail_pick, from_right.astype(jnp.float32), from_left.astype(jnp.float32)
        )
        put(zx, row, jnp.concatenate([middle.astype(jnp.float32), tail], axis=0))

    def first_layer(q, product):
        pre = product + bias_one
        sigma, rest = parts_of(pre)
        row = 2 * q - 3
        inside = jnp.where(lane_half, row_ok(row), row_ok(row + 1))
        kept = sigma * (wide[...] * inside)
        hidden = pre * kept
        slope1[q] = kept + hidden * rest
        put_pair(h1, q, hidden)

    def second_layer(q, product):
        pre = product + bias_two
        sigma, rest = parts_of(pre)
        hidden = pre * sigma
        slope = sigma + hidden * rest
        color = jnp.dot(
            hidden.astype(jnp.bfloat16), rgb_t[...], preferred_element_type=jnp.float32
        )
        residual = mask_t[q] * (color - target_t[q])
        coarse = residual.astype(jnp.bfloat16)
        fine = (residual - coarse.astype(jnp.float32)).astype(jnp.bfloat16)
        grad = jnp.dot(
            jnp.concatenate([coarse, fine], axis=1),
            rgb_b[...],
            preferred_element_type=jnp.float32,
        )
        put_pair(g2, q, grad * slope)

    def back_second(q, product):
        put_pair(g1, q, product * slope1[q + 1])

    half = height // 2
    cuts = (
        (lambda q: conv(zx, q, 0, width), first_layer, 2, 1 + half, half + 3),
        (lambda q: conv(h1, q, 1, width), second_layer, 2, half, half + 2),
        (lambda q: conv(g2, q, 3, width), back_second, 2, half - 1, half + 1),
    )

    results = ((z_ref, latent_out), (m_ref, one_out), (v_ref, two_out), (grad_ref, grad_out))

    def leave(k, q):
        rows = pl.ds(2 * q, 2)
        src, dst = results[k]
        return pltpu.make_async_copy(src.at[rows], dst.at[rows], out_sem.at[k, q])

    for step in range(STEPS):
        last = step == STEPS - 1
        for_each(sides, lambda d: halo_arrival(d, step).wait_recv())

        def own_row(r):
            expand(
                r + HALO, stage[step, r], col_in[step, 0, r], col_in[step, 1, r]
            )

        for r in range(height):
            own_row(r)
        for product, finish, low, high, _ in cuts:
            sweep(product, finish, range(low, high))
        for_each(verticals, lambda d: halo_arrival(d, step).wait_recv())

        def halo_row(r):
            expand(r, row_in[step, 0, r], diag_in[step, 0, 0, r], diag_in[step, 0, 1, r])
            expand(
                r + HALO + height,
                row_in[step, 1, r],
                diag_in[step, 1, 0, r],
                diag_in[step, 1, 1, r],
            )

        for r in range(HALO):
            halo_row(r)
        for product, finish, low, high, count in cuts:
            sweep(product, finish, [*range(low), *range(high, count)])

        if step == 0:
            loads[7].wait()
            loads[8].wait()

        for q in range(half):
            grads = conv(g1, q, 2, breadth)
            for i in range(2):
                r = 2 * q + i
                grad = grads[:, 128 * i : 128 * (i + 1)]
                if last:
                    grad_ref[r] = grad
                    continue
                first = BETA_ONE * m_ref[r] + (1.0 - BETA_ONE) * grad
                second = BETA_TWO * v_ref[r] + (1.0 - BETA_TWO) * grad * grad
                fresh = z_ref[r] - LEARN_RATE * first / (jnp.sqrt(second) + EPSILON)
                m_ref[r] = first
                v_ref[r] = second
                z_ref[r] = fresh
                stage[step + 1, r] = fresh.astype(jnp.bfloat16)
            if last:
                leave(3, q).start()
            elif step == STEPS - 2:
                for k in range(3):
                    leave(k, q).start()
            if not last and 2 * (q + 1) == HALO:
                for_each(uppers, lambda d: halo_copy(d, step + 1).start())
        if not last:
            for_each(lowers + sides, lambda d: halo_copy(d, step + 1).start())

    for step in range(STEPS):
        for_each(DIRS, lambda d: halo_copy(d, step).wait_send())
    for_each(DIRS, lambda d: aux_copy(d).wait_send())
    for k in range(4):
        for q in range(half):
            leave(k, q).wait()


def body(
    sizes,
    latent,
    moment_one,
    moment_two,
    hole_mask,
    target_rgb,
    kernel_one,
    bias_one,
    kernel_two,
    bias_two,
    rgb_weight,
):
    height, breadth, channels = latent.shape
    width = breadth + WRAP
    rows_n, cols_n, cores_n = sizes
    f32, bf16 = jnp.float32, jnp.bfloat16
    far = pl.BlockSpec(memory_space=pltpu.HBM)
    near = pl.BlockSpec(memory_space=pltpu.VMEM)
    tile = jax.ShapeDtypeStruct(latent.shape, f32)
    half = height // 2
    scratch = [
        *[pltpu.VMEM((height, breadth, channels), f32)] * 4,
        pltpu.VMEM((height, breadth), jnp.int32),
        pltpu.VMEM((4, height, breadth), f32),
        pltpu.VMEM((8, 4, height, breadth), f32),
        pltpu.VMEM((STEPS, height, breadth, channels), bf16),
        pltpu.VMEM((STEPS, 2, HALO, breadth, channels), bf16),
        pltpu.VMEM((STEPS, 2, height, WRAP, channels), bf16),
        pltpu.VMEM((STEPS, 2, 2, HALO, WRAP, channels), bf16),
        pltpu.VMEM((height + 8, width, 3 * channels), bf16),
        pltpu.VMEM((height + 6, width, 3 * channels), bf16),
        pltpu.VMEM((height + 4, width, 3 * channels), bf16),
        pltpu.VMEM((height + 2, width, 3 * channels), bf16),
        pltpu.VMEM((half + 3, width, 2 * channels), f32),
        pltpu.VMEM((4, 12 * channels, 2 * channels), bf16),
        pltpu.VMEM((width, 2 * channels), f32),
        pltpu.VMEM((128, 2 * channels), f32),
        pltpu.VMEM((2 * channels, 128), bf16),
        pltpu.VMEM((256, 2 * channels), bf16),
        pltpu.VMEM((half + 2, 16, breadth + 128), f32),
        pltpu.VMEM((half + 2, width, 128), f32),
        pltpu.VMEM((half + 2, width, 128), f32),
        pltpu.SemaphoreType.DMA((9,)),
        pltpu.SemaphoreType.DMA((4, half)),
        pltpu.SemaphoreType.DMA((STEPS, 8)),
        pltpu.SemaphoreType.DMA((STEPS, 8)),
        pltpu.SemaphoreType.DMA((8,)),
        pltpu.SemaphoreType.DMA((8,)),
    ]
    current, first, second, grad = pl.pallas_call(
        functools.partial(kernel, height, breadth, rows_n, cols_n, cores_n),
        out_shape=(tile, tile, tile, tile),
        in_specs=[far] * 7 + [near] * 3,
        out_specs=(far, far, far, far),
        scratch_shapes=scratch,
        compiler_params=pltpu.CompilerParams(
            collective_id=0, has_side_effects=True, vmem_limit_bytes=60 * 1024 * 1024
        ),
        name="inpaint",
    )(
        latent,
        moment_one,
        moment_two,
        hole_mask,
        target_rgb,
        kernel_one.reshape(9 * channels, channels),
        kernel_two.reshape(9 * channels, channels),
        bias_one.reshape(1, channels),
        bias_two.reshape(1, channels),
        rgb_weight,
    )
    first = BETA_ONE * first + (1.0 - BETA_ONE) * grad
    second = BETA_TWO * second + (1.0 - BETA_TWO) * grad * grad
    current = current - LEARN_RATE * first / (jnp.sqrt(second) + EPSILON)
    return current, first, second


def solution(mesh):
    sizes = (mesh.shape["row"], mesh.shape["col"], mesh.shape["cores"])
    tile = P(("parts", "row", "cores"), "col", None)
    return jax.shard_map(
        functools.partial(body, sizes),
        mesh=mesh,
        in_specs=(
            tile,
            tile,
            tile,
            P(("parts", "row", "cores"), "col"),
            P(None, ("parts", "row", "cores"), "col"),
            P(),
            P(),
            P(),
            P(),
            P(),
        ),
        out_specs=(tile, tile, tile),
        check_vma=False,
    )
```

```python
import functools

import jax
import jax.numpy as jnp
from jax import lax
from jax.experimental import pallas as pl
from jax.experimental.pallas import tpu as pltpu
from jax.sharding import PartitionSpec as P

STEPS = 2
BETA_ONE = 0.6
BETA_TWO = 0.9
LEARN_RATE = 0.4
EPSILON = 1e-08

MESH = pl.DeviceIdType.MESH
HALO = 4
WRAP = 16
DIRS = [(-1, 0), (1, 0), (0, -1), (0, 1), (-1, -1), (-1, 1), (1, -1), (1, 1)]


def sweep(tasks):
    ready = None
    for at, (product, finish, places) in enumerate(tasks):
        held = product(places) if at == 0 else ready
        if at + 1 < len(tasks):
            ready = tasks[at + 1][0](tasks[at + 1][2])
        finish(places, held)


def renew(first, second, current, grad):
    first = BETA_ONE * first + (1.0 - BETA_ONE) * grad
    second = BETA_TWO * second + (1.0 - BETA_TWO) * grad * grad
    return first, second, current - LEARN_RATE * first / (jnp.sqrt(second) + EPSILON)


def last_update(half, z_in, m_in, v_in, g_in, z_out, m_out, v_out, z, m, v, g, in_sem, out_sem):
    sources = ((z_in, z), (m_in, m), (v_in, v), (g_in, g))
    targets = ((z, z_out), (m, m_out), (v, v_out))

    def moves(pairs, sem, q):
        rows = pl.ds(2 * q, 2)
        return [
            pltpu.make_async_copy(src.at[rows], dst.at[rows], sem.at[k, q])
            for k, (src, dst) in enumerate(pairs)
        ]

    for q in range(half):
        for c in moves(sources, in_sem, q):
            c.start()
    for q in range(half):
        for c in moves(sources, in_sem, q):
            c.wait()
        rows = pl.ds(2 * q, 2)
        m[rows], v[rows], z[rows] = renew(m[rows], v[rows], z[rows], g[rows])
        for c in moves(targets, out_sem, q):
            c.start()
    for q in range(half):
        for c in moves(targets, out_sem, q):
            c.wait()


def kernel(
    height,
    breadth,
    rows_n,
    cols_n,
    cores_n,
    latent_hbm,
    one_hbm,
    two_hbm,
    mask_hbm,
    target_hbm,
    kone_hbm,
    ktwo_hbm,
    bone_ref,
    btwo_ref,
    rgb_ref,
    latent_out,
    one_out,
    two_out,
    grad_out,
    z_ref,
    m_ref,
    v_ref,
    grad_ref,
    maski,
    aux,
    aux_in,
    stage,
    row_in,
    col_in,
    diag_in,
    zx,
    h1,
    g2,
    g1,
    slope1,
    weights,
    wide,
    rgb_f,
    rgb_t,
    rgb_b,
    target_p,
    target_t,
    mask_t,
    local_sem,
    out_sem,
    send_sem,
    recv_sem,
    aux_send,
    aux_recv,
):
    width = breadth + WRAP
    place = lax.axis_index("row") * cores_n + lax.axis_index("cores")
    col = lax.axis_index("col")
    ranks = rows_n * cores_n

    def there(d):
        dr, dc = d
        ok = None
        if dr:
            ok = place > 0 if dr < 0 else place < ranks - 1
        if dc:
            side = col > 0 if dc < 0 else col < cols_n - 1
            ok = side if ok is None else jnp.logical_and(ok, side)
        return ok

    def peer(d):
        spot = place + d[0]
        return {
            "row": spot // cores_n,
            "cores": lax.rem(spot, cores_n),
            "col": col + d[1],
        }

    live = [d for d in DIRS if not (d[1] and cols_n == 1) and not (d[0] and ranks == 1)]
    slot = {d: i for i, d in enumerate(DIRS)}

    def back(d):
        return (-d[0], -d[1])

    def local(src, dst, i):
        return pltpu.make_async_copy(src, dst, local_sem.at[i])

    loads = [
        local(latent_hbm, z_ref, 0),
        local(target_hbm, aux.at[pl.ds(0, 3)], 1),
        local(mask_hbm, maski, 2),
        local(ktwo_hbm, weights.at[1, pl.ds(0, 9 * 128), pl.ds(0, 128)], 3),
        local(kone_hbm, weights.at[0, pl.ds(0, 9 * 128), pl.ds(0, 128)], 4),
        local(kone_hbm, weights.at[0, pl.ds(384, 9 * 128), pl.ds(128, 128)], 5),
        local(ktwo_hbm, weights.at[1, pl.ds(384, 9 * 128), pl.ds(128, 128)], 6),
        local(one_hbm, m_ref, 7),
        local(two_hbm, v_ref, 8),
    ]
    for c in loads:
        c.start()

    barrier = pltpu.get_barrier_semaphore()
    for d in live:

        @pl.when(there(d))
        def _():
            pl.semaphore_signal(barrier, inc=1, device_id=peer(d), device_id_type=MESH)

    def landing(d, step):
        if d[1] == 0:
            return row_in.at[step, 0 if d[0] < 0 else 1]
        if d[0] == 0:
            return col_in.at[step, 0 if d[1] < 0 else 1]
        return diag_in.at[step, 0 if d[0] < 0 else 1, 0 if d[1] < 0 else 1]

    def outgoing(d, step):
        rows = {0: pl.ds(0, height), -1: pl.ds(0, HALO), 1: pl.ds(height - HALO, HALO)}[d[0]]
        cols = {0: pl.ds(0, breadth), -1: pl.ds(0, WRAP), 1: pl.ds(breadth - WRAP, WRAP)}[d[1]]
        return stage.at[step, rows, cols]

    def halo_copy(d, step):
        return pltpu.make_async_remote_copy(
            src_ref=outgoing(d, step),
            dst_ref=landing(back(d), step),
            send_sem=send_sem.at[step, slot[d]],
            recv_sem=recv_sem.at[step, slot[back(d)]],
            device_id=peer(d),
            device_id_type=MESH,
        )

    def halo_arrival(d, step):
        return pltpu.make_async_remote_copy(
            src_ref=outgoing(back(d), step),
            dst_ref=landing(d, step),
            send_sem=send_sem.at[step, slot[back(d)]],
            recv_sem=recv_sem.at[step, slot[d]],
            device_id=peer(d),
            device_id_type=MESH,
        )

    def aux_copy(d):
        return pltpu.make_async_remote_copy(
            src_ref=aux,
            dst_ref=aux_in.at[slot[back(d)]],
            send_sem=aux_send.at[slot[d]],
            recv_sem=aux_recv.at[slot[back(d)]],
            device_id=peer(d),
            device_id_type=MESH,
        )

    def aux_arrival(d):
        return pltpu.make_async_remote_copy(
            src_ref=aux,
            dst_ref=aux_in.at[slot[d]],
            send_sem=aux_send.at[slot[back(d)]],
            recv_sem=aux_recv.at[slot[d]],
            device_id=peer(d),
            device_id_type=MESH,
        )

    def for_each(dirs, fn):
        for d in dirs:
            if d in live:

                @pl.when(there(d))
                def _():
                    fn(d)

    def clear(d):
        for step in range(STEPS):
            ref = landing(d, step)
            ref[...] = jnp.zeros(ref.shape, ref.dtype)
        aux_in[slot[d]] = jnp.zeros(aux_in.shape[1:], aux_in.dtype)

    for d in DIRS:
        if d not in live:
            clear(d)
        else:

            @pl.when(jnp.logical_not(there(d)))
            def _():
                clear(d)

    sides = [d for d in DIRS if d[0] == 0]
    verticals = [d for d in DIRS if d[0] != 0]
    uppers = [d for d in DIRS if d[0] < 0]
    lowers = [d for d in DIRS if d[0] > 0]

    loads[0].wait()
    stage[0] = z_ref[...].astype(jnp.bfloat16)
    peers = jnp.int32(0)
    for d in live:
        peers = peers + there(d).astype(jnp.int32)
    pl.semaphore_wait(barrier, peers)

    for_each(verticals + sides, lambda d: halo_copy(d, 0).start())
    loads[1].wait()
    loads[2].wait()
    aux[3] = maski[...].astype(jnp.float32)
    for_each(DIRS, lambda d: aux_copy(d).start())

    zero_block = jnp.zeros((384, 128), jnp.bfloat16)
    for i in range(4):
        weights[i, pl.ds(9 * 128, 384), pl.ds(0, 128)] = zero_block
        weights[i, pl.ds(0, 384), pl.ds(128, 128)] = zero_block
    for i in range(3, 7):
        loads[i].wait()

    def turned(layer):
        def flip(tap, carry):
            block = weights[layer, pl.ds(pl.multiple_of(tap * 128, 128), 128), pl.ds(0, 128)]
            block = block.astype(jnp.float32).T.astype(jnp.bfloat16)
            spot = pl.multiple_of((8 - tap) * 128, 128)
            weights[2 + layer, pl.ds(spot, 128), pl.ds(0, 128)] = block
            weights[2 + layer, pl.ds(pl.multiple_of(spot + 384, 128), 128), pl.ds(128, 128)] = block
            return carry

        lax.fori_loop(0, 9, flip, 0)

    turned(1)
    turned(0)

    rgb_f[...] = jnp.zeros(rgb_f.shape, jnp.float32)
    projection = rgb_ref[...].astype(jnp.float32)
    rgb_f[pl.ds(0, 3), pl.ds(0, 128)] = projection
    rgb_f[pl.ds(3, 3), pl.ds(128, 128)] = projection
    full = rgb_f[...]
    rgb_t[...] = full.T.astype(jnp.bfloat16)
    rgb_b[pl.ds(0, 128)] = full.astype(jnp.bfloat16)
    rgb_b[pl.ds(128, 128)] = full.astype(jnp.bfloat16)

    spots = lax.broadcasted_iota(jnp.int32, (width, 256), 0)
    right_ok = (col < cols_n - 1).astype(jnp.float32)
    left_ok = (col > 0).astype(jnp.float32)
    wide[...] = jnp.where(
        spots < breadth, 1.0, jnp.where(spots < breadth + WRAP // 2, right_ok, left_ok)
    )
    up_ok = (place > 0).astype(jnp.float32)
    down_ok = (place < ranks - 1).astype(jnp.float32)

    def row_ok(row):
        return jnp.where(row < 0, up_ok, jnp.where(row >= height, down_ok, 1.0))

    lane_half = lax.broadcasted_iota(jnp.int32, (1, 256), 1) < 128

    for_each(DIRS, lambda d: aux_arrival(d).wait_recv())
    target_p[...] = jnp.zeros(target_p.shape, jnp.float32)
    target_t[...] = jnp.zeros(target_t.shape, jnp.float32)
    mask_t[...] = jnp.zeros(mask_t.shape, jnp.float32)
    pairs_two = (height + 4) // 2
    near = lax.broadcasted_iota(jnp.int32, (4, 128), 1) < WRAP // 2
    for r in range(-2, height + 2):
        if r < 0:
            mid, left, right, at = ((-1, 0), (-1, -1), (-1, 1), height + r)
        elif r < height:
            mid, left, right, at = (None, (0, -1), (0, 1), r)
        else:
            mid, left, right, at = ((1, 0), (1, -1), (1, 1), r - height)
        center = aux[:, at, :] if mid is None else aux_in[slot[mid], :, at, :]
        from_left = aux_in[slot[left], :, at, pl.ds(breadth - 128, 128)]
        from_right = aux_in[slot[right], :, at, pl.ds(0, 128)]
        tail = jnp.where(near, from_right, pltpu.roll(from_left, WRAP, 1))
        q, half = divmod(r + 2, 2)
        for part, lanes in ((center, pl.ds(0, breadth)), (tail, pl.ds(breadth, 128))):
            target_p[q, pl.ds(3 * half, 3), lanes] = part[0:3]
            for k in range(3):
                target_p[q, pl.ds(8 + 3 * half + k, 1), lanes] = part[3:4]
    for q in range(pairs_two):
        target_t[q, :, pl.ds(0, 8)] = target_p[q, pl.ds(0, 8)].T[0:width]
        mask_t[q, :, pl.ds(0, 8)] = target_p[q, pl.ds(8, 8)].T[0:width]

    bias_one = jnp.concatenate([bone_ref[...], bone_ref[...]], axis=1)
    bias_two = jnp.concatenate([btwo_ref[...], btwo_ref[...]], axis=1)

    def put(ref, row, value):
        ref[row, :, pl.ds(0, 128)] = pltpu.roll(value, 1, 0).astype(jnp.bfloat16)
        ref[row, :, pl.ds(128, 128)] = value.astype(jnp.bfloat16)
        ref[row, :, pl.ds(256, 128)] = pltpu.roll(value, width - 1, 0).astype(jnp.bfloat16)

    def put_pair(ref, q, value):
        put(ref, 2 * q, value[:, 0:128])
        put(ref, 2 * q + 1, value[:, 128:256])

    def conv(ref, which, count, places):
        window = jnp.concatenate(
            [
                jnp.concatenate([ref[2 * q + i, pl.ds(0, count), :] for i in range(4)], axis=1)
                for q in places
            ],
            axis=0,
        )
        return jnp.dot(window, weights[which], preferred_element_type=jnp.float32)

    def parts_of(pre):
        turn = 0.5 * jnp.tanh(0.5 * pre)
        return 0.5 + turn, 0.5 - turn

    tail_pick = lax.broadcasted_iota(jnp.int32, (WRAP, 128), 0) < WRAP // 2

    def expand(row, middle, from_left, from_right):
        tail = jnp.where(
            tail_pick, from_right.astype(jnp.float32), from_left.astype(jnp.float32)
        )
        put(zx, row, jnp.concatenate([middle.astype(jnp.float32), tail], axis=0))

    def split(value, count, n):
        return [value[count * i : count * (i + 1)] for i in range(n)]

    def first_layer(places, product):
        for q, part in zip(places, split(product, width, len(places))):
            pre = part + bias_one
            sigma, rest = parts_of(pre)
            row = 2 * q - 3
            inside = wide[...]
            if row < 0 or row + 1 >= height:
                inside = inside * jnp.where(lane_half, row_ok(row), row_ok(row + 1))
            kept = sigma * inside
            hidden = pre * kept
            slope1[q] = kept + hidden * rest
            put_pair(h1, q, hidden)

    def second_layer(places, product):
        n = len(places)
        rounded, slopes = [], []
        for part in split(product, width, n):
            pre = part + bias_two
            sigma, rest = parts_of(pre)
            hidden = pre * sigma
            slopes.append(sigma + hidden * rest)
            rounded.append(hidden.astype(jnp.bfloat16))
        color = jnp.dot(
            jnp.concatenate(rounded, axis=0), rgb_t[...], preferred_element_type=jnp.float32
        )
        terms = []
        for q, part in zip(places, split(color, width, n)):
            residual = mask_t[q] * (part - target_t[q])
            coarse = residual.astype(jnp.bfloat16)
            fine = (residual - coarse.astype(jnp.float32)).astype(jnp.bfloat16)
            terms.append(jnp.concatenate([coarse, fine], axis=1))
        grad = jnp.dot(
            jnp.concatenate(terms, axis=0), rgb_b[...], preferred_element_type=jnp.float32
        )
        for q, part, slope in zip(places, split(grad, width, n), slopes):
            put_pair(g2, q, part * slope)

    def back_second(places, product):
        for q, part in zip(places, split(product, width, len(places))):
            put_pair(g1, q, part * slope1[q + 1])

    half = height // 2
    stages = (
        (functools.partial(conv, zx, 0, width), first_layer, half + 3, 1 + half),
        (functools.partial(conv, h1, 1, width), second_layer, half + 2, half),
        (functools.partial(conv, g2, 3, width), back_second, half + 1, half - 1),
    )

    results = ((z_ref, latent_out), (m_ref, one_out), (v_ref, two_out), (grad_ref, grad_out))

    def leave(k, q):
        rows = pl.ds(2 * q, 2)
        src, dst = results[k]
        return pltpu.make_async_copy(src.at[rows], dst.at[rows], out_sem.at[k, q])

    for step in range(STEPS):
        last = step == STEPS - 1
        for_each(sides, lambda d: halo_arrival(d, step).wait_recv())

        def own_row(r):
            expand(
                r + HALO, stage[step, r], col_in[step, 0, r], col_in[step, 1, r]
            )

        for r in range(height):
            own_row(r)
        tasks = []
        for p, f, _, high in stages[:2]:
            tasks.append((p, f, list(range(2, high - 1))))
            tasks.append((p, f, [high - 1]))
        sweep(tasks)
        p, f, _, high = stages[2]
        sweep([(p, f, list(range(2, high)))])
        for_each(verticals, lambda d: halo_arrival(d, step).wait_recv())

        def halo_row(r):
            expand(r, row_in[step, 0, r], diag_in[step, 0, 0, r], diag_in[step, 0, 1, r])
            expand(
                r + HALO + height,
                row_in[step, 1, r],
                diag_in[step, 1, 0, r],
                diag_in[step, 1, 1, r],
            )

        for r in range(HALO):
            halo_row(r)
        if step == 0:
            loads[7].wait()
            loads[8].wait()

        def update(places, product):
            for q, grads in zip(places, split(product, breadth, len(places))):
                for i in range(2):
                    r = 2 * q + i
                    grad = grads[:, 128 * i : 128 * (i + 1)]
                    if last:
                        grad_ref[r] = grad
                        continue
                    m_ref[r], v_ref[r], z_ref[r] = renew(m_ref[r], v_ref[r], z_ref[r], grad)
                    stage[step + 1, r] = z_ref[r].astype(jnp.bfloat16)
                if last:
                    leave(3, q).start()
                elif step == STEPS - 2:
                    for k in range(3):
                        leave(k, q).start()
            if not last:
                if places[0] == 0:
                    for_each(uppers, lambda d: halo_copy(d, step + 1).start())
                if places[-1] == half - 1:
                    for_each(lowers + sides, lambda d: halo_copy(d, step + 1).start())

        tasks = []
        for p, f, count, high in stages:
            tasks.append((p, f, [0, 1]))
            tasks.append((p, f, list(range(high, count))))
        last_conv = functools.partial(conv, g1, 2, breadth)
        tasks.append((last_conv, update, list(range(half // 2))))
        tasks.append((last_conv, update, list(range(half // 2, half))))
        sweep(tasks)

    for step in range(STEPS):
        for_each(DIRS, lambda d: halo_copy(d, step).wait_send())
    for_each(DIRS, lambda d: aux_copy(d).wait_send())
    for k in range(4):
        for q in range(half):
            leave(k, q).wait()


def body(
    sizes,
    latent,
    moment_one,
    moment_two,
    hole_mask,
    target_rgb,
    kernel_one,
    bias_one,
    kernel_two,
    bias_two,
    rgb_weight,
):
    height, breadth, channels = latent.shape
    width = breadth + WRAP
    rows_n, cols_n, cores_n = sizes
    f32, bf16 = jnp.float32, jnp.bfloat16
    far = pl.BlockSpec(memory_space=pltpu.HBM)
    near = pl.BlockSpec(memory_space=pltpu.VMEM)
    tile = jax.ShapeDtypeStruct(latent.shape, f32)
    half = height // 2
    scratch = [
        *[pltpu.VMEM((height, breadth, channels), f32)] * 4,
        pltpu.VMEM((height, breadth), jnp.int32),
        pltpu.VMEM((4, height, breadth), f32),
        pltpu.VMEM((8, 4, height, breadth), f32),
        pltpu.VMEM((STEPS, height, breadth, channels), bf16),
        pltpu.VMEM((STEPS, 2, HALO, breadth, channels), bf16),
        pltpu.VMEM((STEPS, 2, height, WRAP, channels), bf16),
        pltpu.VMEM((STEPS, 2, 2, HALO, WRAP, channels), bf16),
        pltpu.VMEM((height + 8, width, 3 * channels), bf16),
        pltpu.VMEM((height + 6, width, 3 * channels), bf16),
        pltpu.VMEM((height + 4, width, 3 * channels), bf16),
        pltpu.VMEM((height + 2, width, 3 * channels), bf16),
        pltpu.VMEM((half + 3, width, 2 * channels), f32),
        pltpu.VMEM((4, 12 * channels, 2 * channels), bf16),
        pltpu.VMEM((width, 2 * channels), f32),
        pltpu.VMEM((128, 2 * channels), f32),
        pltpu.VMEM((2 * channels, 128), bf16),
        pltpu.VMEM((256, 2 * channels), bf16),
        pltpu.VMEM((half + 2, 16, breadth + 128), f32),
        pltpu.VMEM((half + 2, width, 128), f32),
        pltpu.VMEM((half + 2, width, 128), f32),
        pltpu.SemaphoreType.DMA((9,)),
        pltpu.SemaphoreType.DMA((4, half)),
        pltpu.SemaphoreType.DMA((STEPS, 8)),
        pltpu.SemaphoreType.DMA((STEPS, 8)),
        pltpu.SemaphoreType.DMA((8,)),
        pltpu.SemaphoreType.DMA((8,)),
    ]
    current, first, second, grad = pl.pallas_call(
        functools.partial(kernel, height, breadth, rows_n, cols_n, cores_n),
        out_shape=(tile, tile, tile, tile),
        in_specs=[far] * 7 + [near] * 3,
        out_specs=(far, far, far, far),
        scratch_shapes=scratch,
        compiler_params=pltpu.CompilerParams(
            collective_id=0, has_side_effects=True, vmem_limit_bytes=60 * 1024 * 1024
        ),
        name="inpaint",
    )(
        latent,
        moment_one,
        moment_two,
        hole_mask,
        target_rgb,
        kernel_one.reshape(9 * channels, channels),
        kernel_two.reshape(9 * channels, channels),
        bias_one.reshape(1, channels),
        bias_two.reshape(1, channels),
        rgb_weight,
    )
    return pl.pallas_call(
        functools.partial(last_update, half),
        out_shape=(tile, tile, tile),
        in_specs=[far] * 4,
        out_specs=(far, far, far),
        scratch_shapes=[
            *[pltpu.VMEM((height, breadth, channels), f32)] * 4,
            pltpu.SemaphoreType.DMA((4, half)),
            pltpu.SemaphoreType.DMA((3, half)),
        ],
        compiler_params=pltpu.CompilerParams(vmem_limit_bytes=60 * 1024 * 1024),
        name="last_update",
    )(current, first, second, grad)


def solution(mesh):
    sizes = (mesh.shape["row"], mesh.shape["col"], mesh.shape["cores"])
    tile = P(("parts", "row", "cores"), "col", None)
    return jax.shard_map(
        functools.partial(body, sizes),
        mesh=mesh,
        in_specs=(
            tile,
            tile,
            tile,
            P(("parts", "row", "cores"), "col"),
            P(None, ("parts", "row", "cores"), "col"),
            P(),
            P(),
            P(),
            P(),
            P(),
        ),
        out_specs=(tile, tile, tile),
        check_vma=False,
    )
```

```python
import functools

import jax
import jax.numpy as jnp
from jax import lax
from jax.experimental import pallas as pl
from jax.experimental.pallas import tpu as pltpu
from jax.sharding import PartitionSpec as P

STEPS = 2
BETA_ONE = 0.6
BETA_TWO = 0.9
LEARN_RATE = 0.4
EPSILON = 1e-08

MESH = pl.DeviceIdType.MESH
HALO = 4
WRAP = 16
DIRS = [(-1, 0), (1, 0), (0, -1), (0, 1), (-1, -1), (-1, 1), (1, -1), (1, 1)]


def sweep(tasks):
    ready = None
    for at, (product, finish, places) in enumerate(tasks):
        held = product(places) if at == 0 else ready
        if at + 1 < len(tasks):
            ready = tasks[at + 1][0](tasks[at + 1][2])
        finish(places, held)


def renew(first, second, current, grad):
    first = BETA_ONE * first + (1.0 - BETA_ONE) * grad
    second = BETA_TWO * second + (1.0 - BETA_TWO) * grad * grad
    return first, second, current - LEARN_RATE * first / (jnp.sqrt(second) + EPSILON)


def last_update(half, z_in, m_in, v_in, g_in, z_out, m_out, v_out, z, m, v, g, in_sem, out_sem):
    sources = ((z_in, z), (m_in, m), (v_in, v), (g_in, g))
    targets = ((z, z_out), (m, m_out), (v, v_out))

    def moves(pairs, sem, q):
        rows = pl.ds(2 * q, 2)
        return [
            pltpu.make_async_copy(src.at[rows], dst.at[rows], sem.at[k, q])
            for k, (src, dst) in enumerate(pairs)
        ]

    for q in range(half):
        for c in moves(sources, in_sem, q):
            c.start()
    for q in range(half):
        for c in moves(sources, in_sem, q):
            c.wait()
        rows = pl.ds(2 * q, 2)
        m[rows], v[rows], z[rows] = renew(m[rows], v[rows], z[rows], g[rows])
        for c in moves(targets, out_sem, q):
            c.start()
    for q in range(half):
        for c in moves(targets, out_sem, q):
            c.wait()


def kernel(
    height,
    breadth,
    rows_n,
    cols_n,
    cores_n,
    latent_hbm,
    one_hbm,
    two_hbm,
    mask_hbm,
    target_hbm,
    kone_hbm,
    ktwo_hbm,
    bone_ref,
    btwo_ref,
    rgb_ref,
    latent_out,
    one_out,
    two_out,
    grad_out,
    z_ref,
    m_ref,
    v_ref,
    grad_ref,
    maski,
    aux,
    aux_in,
    stage,
    row_in,
    col_in,
    diag_in,
    zx,
    h1,
    g2,
    g1,
    slope1,
    weights,
    wide,
    rgb_f,
    rgb_t,
    rgb_b,
    target_p,
    target_t,
    mask_t,
    local_sem,
    out_sem,
    send_sem,
    recv_sem,
    aux_send,
    aux_recv,
):
    width = breadth + WRAP
    place = lax.axis_index("row") * cores_n + lax.axis_index("cores")
    col = lax.axis_index("col")
    ranks = rows_n * cores_n

    def there(d):
        dr, dc = d
        ok = None
        if dr:
            ok = place > 0 if dr < 0 else place < ranks - 1
        if dc:
            side = col > 0 if dc < 0 else col < cols_n - 1
            ok = side if ok is None else jnp.logical_and(ok, side)
        return ok

    def peer(d):
        spot = place + d[0]
        return {
            "row": spot // cores_n,
            "cores": lax.rem(spot, cores_n),
            "col": col + d[1],
        }

    live = [d for d in DIRS if not (d[1] and cols_n == 1) and not (d[0] and ranks == 1)]
    slot = {d: i for i, d in enumerate(DIRS)}

    def back(d):
        return (-d[0], -d[1])

    def local(src, dst, i):
        return pltpu.make_async_copy(src, dst, local_sem.at[i])

    loads = [
        local(latent_hbm, z_ref, 0),
        local(target_hbm, aux.at[pl.ds(0, 3)], 1),
        local(mask_hbm, maski, 2),
        local(kone_hbm, weights.at[0, pl.ds(0, 9 * 128), pl.ds(0, 128)], 3),
        local(ktwo_hbm, weights.at[1, pl.ds(0, 9 * 128), pl.ds(0, 128)], 4),
        local(one_hbm, m_ref, 5),
        local(two_hbm, v_ref, 6),
    ]
    for c in loads[:5]:
        c.start()

    barrier = pltpu.get_barrier_semaphore()
    for d in live:

        @pl.when(there(d))
        def _():
            pl.semaphore_signal(barrier, inc=1, device_id=peer(d), device_id_type=MESH)

    def landing(d, step):
        if d[1] == 0:
            return row_in.at[step, 0 if d[0] < 0 else 1]
        if d[0] == 0:
            return col_in.at[step, 0 if d[1] < 0 else 1]
        return diag_in.at[step, 0 if d[0] < 0 else 1, 0 if d[1] < 0 else 1]

    def outgoing(d, step):
        rows = {0: pl.ds(0, height), -1: pl.ds(0, HALO), 1: pl.ds(height - HALO, HALO)}[d[0]]
        cols = {0: pl.ds(0, breadth), -1: pl.ds(0, WRAP), 1: pl.ds(breadth - WRAP, WRAP)}[d[1]]
        return stage.at[step, rows, cols]

    def halo_copy(d, step):
        return pltpu.make_async_remote_copy(
            src_ref=outgoing(d, step),
            dst_ref=landing(back(d), step),
            send_sem=send_sem.at[step, slot[d]],
            recv_sem=recv_sem.at[step, slot[back(d)]],
            device_id=peer(d),
            device_id_type=MESH,
        )

    def halo_arrival(d, step):
        return pltpu.make_async_remote_copy(
            src_ref=outgoing(back(d), step),
            dst_ref=landing(d, step),
            send_sem=send_sem.at[step, slot[back(d)]],
            recv_sem=recv_sem.at[step, slot[d]],
            device_id=peer(d),
            device_id_type=MESH,
        )

    def aux_copy(d):
        return pltpu.make_async_remote_copy(
            src_ref=aux,
            dst_ref=aux_in.at[slot[back(d)]],
            send_sem=aux_send.at[slot[d]],
            recv_sem=aux_recv.at[slot[back(d)]],
            device_id=peer(d),
            device_id_type=MESH,
        )

    def aux_arrival(d):
        return pltpu.make_async_remote_copy(
            src_ref=aux,
            dst_ref=aux_in.at[slot[d]],
            send_sem=aux_send.at[slot[back(d)]],
            recv_sem=aux_recv.at[slot[d]],
            device_id=peer(d),
            device_id_type=MESH,
        )

    def for_each(dirs, fn):
        for d in dirs:
            if d in live:

                @pl.when(there(d))
                def _():
                    fn(d)

    def clear(d):
        for step in range(STEPS):
            ref = landing(d, step)
            ref[...] = jnp.zeros(ref.shape, ref.dtype)
        aux_in[slot[d]] = jnp.zeros(aux_in.shape[1:], aux_in.dtype)

    for d in DIRS:
        if d not in live:
            clear(d)
        else:

            @pl.when(jnp.logical_not(there(d)))
            def _():
                clear(d)

    sides = [d for d in DIRS if d[0] == 0]
    verticals = [d for d in DIRS if d[0] != 0]
    uppers = [d for d in DIRS if d[0] < 0]
    lowers = [d for d in DIRS if d[0] > 0]

    loads[0].wait()
    stage[0] = z_ref[...].astype(jnp.bfloat16)
    peers = jnp.int32(0)
    for d in live:
        peers = peers + there(d).astype(jnp.int32)
    pl.semaphore_wait(barrier, peers)

    for_each(verticals + sides, lambda d: halo_copy(d, 0).start())
    loads[1].wait()
    loads[2].wait()
    aux[3] = maski[...].astype(jnp.float32)
    for_each(DIRS, lambda d: aux_copy(d).start())

    loads[3].wait()
    loads[4].wait()
    loads[5].start()
    loads[6].start()
    for_each(DIRS, lambda d: aux_arrival(d).wait_recv())
    for_each(sides, lambda d: halo_arrival(d, 0).wait_recv())

    zero_block = jnp.zeros((384, 128), jnp.bfloat16)
    for i in range(4):
        weights[i, pl.ds(9 * 128, 384), pl.ds(0, 128)] = zero_block
        weights[i, pl.ds(0, 384), pl.ds(128, 128)] = zero_block
    for layer in range(2):
        weights[layer, pl.ds(384, 9 * 128), pl.ds(128, 128)] = weights[
            layer, pl.ds(0, 9 * 128), pl.ds(0, 128)
        ]

    for layer in (1, 0):
        for tap in range(9):
            block = weights[layer, pl.ds(tap * 128, 128), pl.ds(0, 128)]
            block = block.astype(jnp.float32).T.astype(jnp.bfloat16)
            spot = (8 - tap) * 128
            weights[2 + layer, pl.ds(spot, 128), pl.ds(0, 128)] = block
            weights[2 + layer, pl.ds(spot + 384, 128), pl.ds(128, 128)] = block

    rgb_f[...] = jnp.zeros(rgb_f.shape, jnp.float32)
    projection = rgb_ref[...].astype(jnp.float32)
    rgb_f[pl.ds(0, 3), pl.ds(0, 128)] = projection
    rgb_f[pl.ds(3, 3), pl.ds(128, 128)] = projection
    full = rgb_f[...]
    rgb_t[...] = full.T.astype(jnp.bfloat16)
    rgb_b[pl.ds(0, 128)] = full.astype(jnp.bfloat16)
    rgb_b[pl.ds(128, 128)] = full.astype(jnp.bfloat16)

    spots = lax.broadcasted_iota(jnp.int32, (width, 256), 0)
    right_ok = (col < cols_n - 1).astype(jnp.float32)
    left_ok = (col > 0).astype(jnp.float32)
    wide[...] = jnp.where(
        spots < breadth, 1.0, jnp.where(spots < breadth + WRAP // 2, right_ok, left_ok)
    )
    up_ok = (place > 0).astype(jnp.float32)
    down_ok = (place < ranks - 1).astype(jnp.float32)

    def row_ok(row):
        return jnp.where(row < 0, up_ok, jnp.where(row >= height, down_ok, 1.0))

    lane_half = lax.broadcasted_iota(jnp.int32, (1, 256), 1) < 128

    target_p[...] = jnp.zeros(target_p.shape, jnp.float32)
    target_t[...] = jnp.zeros(target_t.shape, jnp.float32)
    mask_t[...] = jnp.zeros(mask_t.shape, jnp.float32)
    pairs_two = (height + 4) // 2
    near = lax.broadcasted_iota(jnp.int32, (4, 128), 1) < WRAP // 2
    for r in range(-2, height + 2):
        if r < 0:
            mid, left, right, at = ((-1, 0), (-1, -1), (-1, 1), height + r)
        elif r < height:
            mid, left, right, at = (None, (0, -1), (0, 1), r)
        else:
            mid, left, right, at = ((1, 0), (1, -1), (1, 1), r - height)
        center = aux[:, at, :] if mid is None else aux_in[slot[mid], :, at, :]
        from_left = aux_in[slot[left], :, at, pl.ds(breadth - 128, 128)]
        from_right = aux_in[slot[right], :, at, pl.ds(0, 128)]
        tail = jnp.where(near, from_right, pltpu.roll(from_left, WRAP, 1))
        q, half = divmod(r + 2, 2)
        for part, lanes in ((center, pl.ds(0, breadth)), (tail, pl.ds(breadth, 128))):
            target_p[q, pl.ds(3 * half, 3), lanes] = part[0:3]
            for k in range(3):
                target_p[q, pl.ds(8 + 3 * half + k, 1), lanes] = part[3:4]
    for q in range(pairs_two):
        target_t[q, :, pl.ds(0, 8)] = target_p[q, pl.ds(0, 8)].T[0:width]
        mask_t[q, :, pl.ds(0, 8)] = target_p[q, pl.ds(8, 8)].T[0:width]

    bias_one = jnp.concatenate([bone_ref[...], bone_ref[...]], axis=1)
    bias_two = jnp.concatenate([btwo_ref[...], btwo_ref[...]], axis=1)

    def put(ref, row, value):
        ref[row, :, pl.ds(0, 128)] = pltpu.roll(value, 1, 0).astype(jnp.bfloat16)
        ref[row, :, pl.ds(128, 128)] = value.astype(jnp.bfloat16)
        ref[row, :, pl.ds(256, 128)] = pltpu.roll(value, width - 1, 0).astype(jnp.bfloat16)

    def put_pair(ref, q, value):
        put(ref, 2 * q, value[:, 0:128])
        put(ref, 2 * q + 1, value[:, 128:256])

    def conv(ref, which, count, places):
        window = jnp.concatenate(
            [
                jnp.concatenate([ref[2 * q + i, pl.ds(0, count), :] for i in range(4)], axis=1)
                for q in places
            ],
            axis=0,
        )
        return jnp.dot(window, weights[which], preferred_element_type=jnp.float32)

    def parts_of(pre):
        turn = 0.5 * jnp.tanh(0.5 * pre)
        return 0.5 + turn, 0.5 - turn

    tail_pick = lax.broadcasted_iota(jnp.int32, (WRAP, 128), 0) < WRAP // 2

    def expand(row, middle, from_left, from_right):
        tail = jnp.where(
            tail_pick, from_right.astype(jnp.float32), from_left.astype(jnp.float32)
        )
        put(zx, row, jnp.concatenate([middle.astype(jnp.float32), tail], axis=0))

    def split(value, count, n):
        return [value[count * i : count * (i + 1)] for i in range(n)]

    def first_layer(places, product):
        for q, part in zip(places, split(product, width, len(places))):
            pre = part + bias_one
            sigma, rest = parts_of(pre)
            row = 2 * q - 3
            inside = wide[...]
            if row < 0 or row + 1 >= height:
                inside = inside * jnp.where(lane_half, row_ok(row), row_ok(row + 1))
            kept = sigma * inside
            hidden = pre * kept
            slope1[q] = kept + hidden * rest
            put_pair(h1, q, hidden)

    def second_layer(places, product):
        n = len(places)
        rounded, slopes = [], []
        for part in split(product, width, n):
            pre = part + bias_two
            sigma, rest = parts_of(pre)
            hidden = pre * sigma
            slopes.append(sigma + hidden * rest)
            rounded.append(hidden.astype(jnp.bfloat16))
        color = jnp.dot(
            jnp.concatenate(rounded, axis=0), rgb_t[...], preferred_element_type=jnp.float32
        )
        terms = []
        for q, part in zip(places, split(color, width, n)):
            residual = mask_t[q] * (part - target_t[q])
            coarse = residual.astype(jnp.bfloat16)
            fine = (residual - coarse.astype(jnp.float32)).astype(jnp.bfloat16)
            terms.append(jnp.concatenate([coarse, fine], axis=1))
        grad = jnp.dot(
            jnp.concatenate(terms, axis=0), rgb_b[...], preferred_element_type=jnp.float32
        )
        for q, part, slope in zip(places, split(grad, width, n), slopes):
            put_pair(g2, q, part * slope)

    def back_second(places, product):
        for q, part in zip(places, split(product, width, len(places))):
            put_pair(g1, q, part * slope1[q + 1])

    half = height // 2
    stages = (
        (functools.partial(conv, zx, 0, width), first_layer, half + 3, 1 + half),
        (functools.partial(conv, h1, 1, width), second_layer, half + 2, half),
        (functools.partial(conv, g2, 3, width), back_second, half + 1, half - 1),
    )

    results = ((z_ref, latent_out), (m_ref, one_out), (v_ref, two_out), (grad_ref, grad_out))

    def leave(k, q):
        rows = pl.ds(2 * q, 2)
        src, dst = results[k]
        return pltpu.make_async_copy(src.at[rows], dst.at[rows], out_sem.at[k, q])

    for step in range(STEPS):
        last = step == STEPS - 1
        if step > 0:
            for_each(sides, lambda d: halo_arrival(d, step).wait_recv())

        def own_row(r):
            expand(
                r + HALO, stage[step, r], col_in[step, 0, r], col_in[step, 1, r]
            )

        for r in range(height):
            own_row(r)
        tasks = []
        for p, f, _, high in stages[:2]:
            tasks.append((p, f, list(range(2, high - 1))))
            tasks.append((p, f, [high - 1]))
        sweep(tasks)
        p, f, _, high = stages[2]
        sweep([(p, f, list(range(2, high)))])
        for_each(verticals, lambda d: halo_arrival(d, step).wait_recv())

        def halo_row(r):
            expand(r, row_in[step, 0, r], diag_in[step, 0, 0, r], diag_in[step, 0, 1, r])
            expand(
                r + HALO + height,
                row_in[step, 1, r],
                diag_in[step, 1, 0, r],
                diag_in[step, 1, 1, r],
            )

        for r in range(HALO):
            halo_row(r)
        if step == 0:
            loads[5].wait()
            loads[6].wait()

        def update(places, product):
            for q, grads in zip(places, split(product, breadth, len(places))):
                for i in range(2):
                    r = 2 * q + i
                    grad = grads[:, 128 * i : 128 * (i + 1)]
                    if last:
                        grad_ref[r] = grad
                        continue
                    m_ref[r], v_ref[r], z_ref[r] = renew(m_ref[r], v_ref[r], z_ref[r], grad)
                    stage[step + 1, r] = z_ref[r].astype(jnp.bfloat16)
                if last:
                    leave(3, q).start()
                elif step == STEPS - 2:
                    for k in range(3):
                        leave(k, q).start()
            if not last:
                if places[0] == 0:
                    for_each(uppers, lambda d: halo_copy(d, step + 1).start())
                if places[-1] == half - 1:
                    for_each(lowers + sides, lambda d: halo_copy(d, step + 1).start())

        tasks = []
        for p, f, count, high in stages:
            tasks.append((p, f, [0, 1]))
            tasks.append((p, f, list(range(high, count))))
        last_conv = functools.partial(conv, g1, 2, breadth)
        tasks.append((last_conv, update, list(range(half // 2))))
        tasks.append((last_conv, update, list(range(half // 2, half))))
        sweep(tasks)

    for step in range(STEPS):
        for_each(DIRS, lambda d: halo_copy(d, step).wait_send())
    for_each(DIRS, lambda d: aux_copy(d).wait_send())
    for k in range(4):
        for q in range(half):
            leave(k, q).wait()


def body(
    sizes,
    latent,
    moment_one,
    moment_two,
    hole_mask,
    target_rgb,
    kernel_one,
    bias_one,
    kernel_two,
    bias_two,
    rgb_weight,
):
    height, breadth, channels = latent.shape
    width = breadth + WRAP
    rows_n, cols_n, cores_n = sizes
    f32, bf16 = jnp.float32, jnp.bfloat16
    far = pl.BlockSpec(memory_space=pltpu.HBM)
    near = pl.BlockSpec(memory_space=pltpu.VMEM)
    tile = jax.ShapeDtypeStruct(latent.shape, f32)
    half = height // 2
    scratch = [
        *[pltpu.VMEM((height, breadth, channels), f32)] * 4,
        pltpu.VMEM((height, breadth), jnp.int32),
        pltpu.VMEM((4, height, breadth), f32),
        pltpu.VMEM((8, 4, height, breadth), f32),
        pltpu.VMEM((STEPS, height, breadth, channels), bf16),
        pltpu.VMEM((STEPS, 2, HALO, breadth, channels), bf16),
        pltpu.VMEM((STEPS, 2, height, WRAP, channels), bf16),
        pltpu.VMEM((STEPS, 2, 2, HALO, WRAP, channels), bf16),
        pltpu.VMEM((height + 8, width, 3 * channels), bf16),
        pltpu.VMEM((height + 6, width, 3 * channels), bf16),
        pltpu.VMEM((height + 4, width, 3 * channels), bf16),
        pltpu.VMEM((height + 2, width, 3 * channels), bf16),
        pltpu.VMEM((half + 3, width, 2 * channels), f32),
        pltpu.VMEM((4, 12 * channels, 2 * channels), bf16),
        pltpu.VMEM((width, 2 * channels), f32),
        pltpu.VMEM((128, 2 * channels), f32),
        pltpu.VMEM((2 * channels, 128), bf16),
        pltpu.VMEM((256, 2 * channels), bf16),
        pltpu.VMEM((half + 2, 16, breadth + 128), f32),
        pltpu.VMEM((half + 2, width, 128), f32),
        pltpu.VMEM((half + 2, width, 128), f32),
        pltpu.SemaphoreType.DMA((7,)),
        pltpu.SemaphoreType.DMA((4, half)),
        pltpu.SemaphoreType.DMA((STEPS, 8)),
        pltpu.SemaphoreType.DMA((STEPS, 8)),
        pltpu.SemaphoreType.DMA((8,)),
        pltpu.SemaphoreType.DMA((8,)),
    ]
    current, first, second, grad = pl.pallas_call(
        functools.partial(kernel, height, breadth, rows_n, cols_n, cores_n),
        out_shape=(tile, tile, tile, tile),
        in_specs=[far] * 7 + [near] * 3,
        out_specs=(far, far, far, far),
        scratch_shapes=scratch,
        compiler_params=pltpu.CompilerParams(
            collective_id=0, has_side_effects=True, vmem_limit_bytes=60 * 1024 * 1024
        ),
        name="inpaint",
    )(
        latent,
        moment_one,
        moment_two,
        hole_mask,
        target_rgb,
        kernel_one.reshape(9 * channels, channels),
        kernel_two.reshape(9 * channels, channels),
        bias_one.reshape(1, channels),
        bias_two.reshape(1, channels),
        rgb_weight,
    )
    return pl.pallas_call(
        functools.partial(last_update, half),
        out_shape=(tile, tile, tile),
        in_specs=[far] * 4,
        out_specs=(far, far, far),
        scratch_shapes=[
            *[pltpu.VMEM((height, breadth, channels), f32)] * 4,
            pltpu.SemaphoreType.DMA((4, half)),
            pltpu.SemaphoreType.DMA((3, half)),
        ],
        compiler_params=pltpu.CompilerParams(vmem_limit_bytes=60 * 1024 * 1024),
        name="last_update",
    )(current, first, second, grad)


def solution(mesh):
    sizes = (mesh.shape["row"], mesh.shape["col"], mesh.shape["cores"])
    tile = P(("parts", "row", "cores"), "col", None)
    return jax.shard_map(
        functools.partial(body, sizes),
        mesh=mesh,
        in_specs=(
            tile,
            tile,
            tile,
            P(("parts", "row", "cores"), "col"),
            P(None, ("parts", "row", "cores"), "col"),
            P(),
            P(),
            P(),
            P(),
            P(),
        ),
        out_specs=(tile, tile, tile),
        check_vma=False,
    )
```

```python
import functools

import jax
import jax.numpy as jnp
from jax import lax
from jax.experimental import pallas as pl
from jax.experimental.pallas import tpu as pltpu
from jax.sharding import PartitionSpec as P

STEPS = 2
BETA_ONE = 0.6
BETA_TWO = 0.9
LEARN_RATE = 0.4
EPSILON = 1e-08

MESH = pl.DeviceIdType.MESH
HALO = 4
WRAP = 16
DIRS = [(-1, 0), (1, 0), (0, -1), (0, 1), (-1, -1), (-1, 1), (1, -1), (1, 1)]


def sweep(tasks):
    ready = None
    for at, (product, finish, places) in enumerate(tasks):
        held = product(places) if at == 0 else ready
        if at + 1 < len(tasks):
            ready = tasks[at + 1][0](tasks[at + 1][2])
        finish(places, held)


def renew(first, second, current, grad):
    first = BETA_ONE * first + (1.0 - BETA_ONE) * grad
    second = BETA_TWO * second + (1.0 - BETA_TWO) * grad * grad
    return first, second, current - LEARN_RATE * first / (jnp.sqrt(second) + EPSILON)


def last_update(half, z_in, m_in, v_in, g_in, z_out, m_out, v_out, z, m, v, g, in_sem, out_sem):
    sources = ((z_in, z), (m_in, m), (v_in, v), (g_in, g))
    targets = ((z, z_out), (m, m_out), (v, v_out))

    def moves(pairs, sem, q):
        rows = pl.ds(2 * q, 2)
        return [
            pltpu.make_async_copy(src.at[rows], dst.at[rows], sem.at[k, q])
            for k, (src, dst) in enumerate(pairs)
        ]

    for q in range(half):
        for c in moves(sources, in_sem, q):
            c.start()
    for q in range(half):
        for c in moves(sources, in_sem, q):
            c.wait()
        rows = pl.ds(2 * q, 2)
        m[rows], v[rows], z[rows] = renew(m[rows], v[rows], z[rows], g[rows])
        for c in moves(targets, out_sem, q):
            c.start()
    for q in range(half):
        for c in moves(targets, out_sem, q):
            c.wait()


def kernel(
    height,
    breadth,
    rows_n,
    cols_n,
    cores_n,
    latent_hbm,
    one_hbm,
    two_hbm,
    mask_hbm,
    target_hbm,
    kone_hbm,
    ktwo_hbm,
    bone_ref,
    btwo_ref,
    rgb_ref,
    latent_out,
    one_out,
    two_out,
    grad_out,
    z_ref,
    m_ref,
    v_ref,
    grad_ref,
    maski,
    aux,
    aux_in,
    stage,
    row_in,
    col_in,
    diag_in,
    zx,
    h1,
    g2,
    g1,
    slope1,
    weights,
    wide,
    rgb_f,
    rgb_t,
    rgb_b,
    target_p,
    target_t,
    mask_t,
    local_sem,
    out_sem,
    send_sem,
    recv_sem,
    aux_send,
    aux_recv,
):
    width = breadth + WRAP
    place = lax.axis_index("row") * cores_n + lax.axis_index("cores")
    col = lax.axis_index("col")
    ranks = rows_n * cores_n

    def there(d):
        dr, dc = d
        ok = None
        if dr:
            ok = place > 0 if dr < 0 else place < ranks - 1
        if dc:
            side = col > 0 if dc < 0 else col < cols_n - 1
            ok = side if ok is None else jnp.logical_and(ok, side)
        return ok

    def peer(d):
        spot = place + d[0]
        return {
            "row": spot // cores_n,
            "cores": lax.rem(spot, cores_n),
            "col": col + d[1],
        }

    live = [d for d in DIRS if not (d[1] and cols_n == 1) and not (d[0] and ranks == 1)]
    slot = {d: i for i, d in enumerate(DIRS)}

    def back(d):
        return (-d[0], -d[1])

    def local(src, dst, i):
        return pltpu.make_async_copy(src, dst, local_sem.at[i])

    loads = [
        local(latent_hbm, z_ref, 0),
        local(target_hbm, aux.at[pl.ds(0, 3)], 1),
        local(mask_hbm, maski, 2),
        local(kone_hbm, weights.at[0, pl.ds(0, 9 * 128), pl.ds(0, 128)], 3),
        local(ktwo_hbm, weights.at[1, pl.ds(0, 9 * 128), pl.ds(0, 128)], 4),
        local(one_hbm, m_ref, 5),
        local(two_hbm, v_ref, 6),
    ]
    for c in loads[:5]:
        c.start()

    barrier = pltpu.get_barrier_semaphore()
    for d in live:

        @pl.when(there(d))
        def _():
            pl.semaphore_signal(barrier, inc=1, device_id=peer(d), device_id_type=MESH)

    def landing(d, step):
        if d[1] == 0:
            return row_in.at[step, 0 if d[0] < 0 else 1]
        if d[0] == 0:
            return col_in.at[step, 0 if d[1] < 0 else 1]
        return diag_in.at[step, 0 if d[0] < 0 else 1, 0 if d[1] < 0 else 1]

    def outgoing(d, step):
        rows = {0: pl.ds(0, height), -1: pl.ds(0, HALO), 1: pl.ds(height - HALO, HALO)}[d[0]]
        cols = {0: pl.ds(0, breadth), -1: pl.ds(0, WRAP), 1: pl.ds(breadth - WRAP, WRAP)}[d[1]]
        return stage.at[step, rows, cols]

    def halo_copy(d, step):
        return pltpu.make_async_remote_copy(
            src_ref=outgoing(d, step),
            dst_ref=landing(back(d), step),
            send_sem=send_sem.at[step, slot[d]],
            recv_sem=recv_sem.at[step, slot[back(d)]],
            device_id=peer(d),
            device_id_type=MESH,
        )

    def halo_arrival(d, step):
        return pltpu.make_async_remote_copy(
            src_ref=outgoing(back(d), step),
            dst_ref=landing(d, step),
            send_sem=send_sem.at[step, slot[back(d)]],
            recv_sem=recv_sem.at[step, slot[d]],
            device_id=peer(d),
            device_id_type=MESH,
        )

    def aux_copy(d):
        return pltpu.make_async_remote_copy(
            src_ref=aux,
            dst_ref=aux_in.at[slot[back(d)]],
            send_sem=aux_send.at[slot[d]],
            recv_sem=aux_recv.at[slot[back(d)]],
            device_id=peer(d),
            device_id_type=MESH,
        )

    def aux_arrival(d):
        return pltpu.make_async_remote_copy(
            src_ref=aux,
            dst_ref=aux_in.at[slot[d]],
            send_sem=aux_send.at[slot[back(d)]],
            recv_sem=aux_recv.at[slot[d]],
            device_id=peer(d),
            device_id_type=MESH,
        )

    def for_each(dirs, fn):
        for d in dirs:
            if d in live:

                @pl.when(there(d))
                def _():
                    fn(d)

    def clear(d):
        for step in range(STEPS):
            ref = landing(d, step)
            ref[...] = jnp.zeros(ref.shape, ref.dtype)
        aux_in[slot[d]] = jnp.zeros(aux_in.shape[1:], aux_in.dtype)

    for d in DIRS:
        if d not in live:
            clear(d)
        else:

            @pl.when(jnp.logical_not(there(d)))
            def _():
                clear(d)

    sides = [d for d in DIRS if d[0] == 0]
    verticals = [d for d in DIRS if d[0] != 0]
    uppers = [d for d in DIRS if d[0] < 0]
    lowers = [d for d in DIRS if d[0] > 0]

    loads[0].wait()
    stage[0] = z_ref[...].astype(jnp.bfloat16)
    peers = jnp.int32(0)
    for d in live:
        peers = peers + there(d).astype(jnp.int32)
    pl.semaphore_wait(barrier, peers)

    for_each(verticals + sides, lambda d: halo_copy(d, 0).start())
    loads[1].wait()
    loads[2].wait()
    aux[3] = maski[...].astype(jnp.float32)
    for_each(DIRS, lambda d: aux_copy(d).start())

    loads[3].wait()
    loads[4].wait()
    loads[5].start()
    loads[6].start()

    zero_block = jnp.zeros((384, 128), jnp.bfloat16)
    for i in range(4):
        weights[i, pl.ds(9 * 128, 384), pl.ds(0, 128)] = zero_block
        weights[i, pl.ds(0, 384), pl.ds(128, 128)] = zero_block
    for layer in range(2):
        weights[layer, pl.ds(384, 9 * 128), pl.ds(128, 128)] = weights[
            layer, pl.ds(0, 9 * 128), pl.ds(0, 128)
        ]

    for layer in (1, 0):
        for tap in range(9):
            block = weights[layer, pl.ds(tap * 128, 128), pl.ds(0, 128)]
            block = block.astype(jnp.float32).T.astype(jnp.bfloat16)
            spot = (8 - tap) * 128
            weights[2 + layer, pl.ds(spot, 128), pl.ds(0, 128)] = block
            weights[2 + layer, pl.ds(spot + 384, 128), pl.ds(128, 128)] = block

    rgb_f[...] = jnp.zeros(rgb_f.shape, jnp.float32)
    projection = rgb_ref[...].astype(jnp.float32)
    rgb_f[pl.ds(0, 3), pl.ds(0, 128)] = projection
    rgb_f[pl.ds(3, 3), pl.ds(128, 128)] = projection
    full = rgb_f[...]
    rgb_t[...] = full.T.astype(jnp.bfloat16)
    rgb_b[pl.ds(0, 128)] = full.astype(jnp.bfloat16)
    rgb_b[pl.ds(128, 128)] = full.astype(jnp.bfloat16)

    spots = lax.broadcasted_iota(jnp.int32, (width, 256), 0)
    right_ok = (col < cols_n - 1).astype(jnp.float32)
    left_ok = (col > 0).astype(jnp.float32)
    wide[...] = jnp.where(
        spots < breadth, 1.0, jnp.where(spots < breadth + WRAP // 2, right_ok, left_ok)
    )
    up_ok = (place > 0).astype(jnp.float32)
    down_ok = (place < ranks - 1).astype(jnp.float32)

    def row_ok(row):
        return jnp.where(row < 0, up_ok, jnp.where(row >= height, down_ok, 1.0))

    lane_half = lax.broadcasted_iota(jnp.int32, (1, 256), 1) < 128

    for_each(DIRS, lambda d: aux_arrival(d).wait_recv())
    for_each(sides, lambda d: halo_arrival(d, 0).wait_recv())

    target_p[...] = jnp.zeros(target_p.shape, jnp.float32)
    target_t[...] = jnp.zeros(target_t.shape, jnp.float32)
    mask_t[...] = jnp.zeros(mask_t.shape, jnp.float32)
    pairs_two = (height + 4) // 2
    near = lax.broadcasted_iota(jnp.int32, (4, 128), 1) < WRAP // 2
    for r in range(-2, height + 2):
        if r < 0:
            mid, left, right, at = ((-1, 0), (-1, -1), (-1, 1), height + r)
        elif r < height:
            mid, left, right, at = (None, (0, -1), (0, 1), r)
        else:
            mid, left, right, at = ((1, 0), (1, -1), (1, 1), r - height)
        center = aux[:, at, :] if mid is None else aux_in[slot[mid], :, at, :]
        from_left = aux_in[slot[left], :, at, pl.ds(breadth - 128, 128)]
        from_right = aux_in[slot[right], :, at, pl.ds(0, 128)]
        tail = jnp.where(near, from_right, pltpu.roll(from_left, WRAP, 1))
        q, half = divmod(r + 2, 2)
        for part, lanes in ((center, pl.ds(0, breadth)), (tail, pl.ds(breadth, 128))):
            target_p[q, pl.ds(3 * half, 3), lanes] = part[0:3]
            for k in range(3):
                target_p[q, pl.ds(8 + 3 * half + k, 1), lanes] = part[3:4]
    for q in range(pairs_two):
        target_t[q, :, pl.ds(0, 8)] = target_p[q, pl.ds(0, 8)].T[0:width]
        mask_t[q, :, pl.ds(0, 8)] = target_p[q, pl.ds(8, 8)].T[0:width]

    bias_one = jnp.concatenate([bone_ref[...], bone_ref[...]], axis=1)
    bias_two = jnp.concatenate([btwo_ref[...], btwo_ref[...]], axis=1)

    def put(ref, row, value):
        ref[row, :, pl.ds(0, 128)] = pltpu.roll(value, 1, 0).astype(jnp.bfloat16)
        ref[row, :, pl.ds(128, 128)] = value.astype(jnp.bfloat16)
        ref[row, :, pl.ds(256, 128)] = pltpu.roll(value, width - 1, 0).astype(jnp.bfloat16)

    def put_pair(ref, q, value):
        put(ref, 2 * q, value[:, 0:128])
        put(ref, 2 * q + 1, value[:, 128:256])

    def conv(ref, which, count, places):
        window = jnp.concatenate(
            [
                jnp.concatenate([ref[2 * q + i, pl.ds(0, count), :] for i in range(4)], axis=1)
                for q in places
            ],
            axis=0,
        )
        return jnp.dot(window, weights[which], preferred_element_type=jnp.float32)

    def parts_of(pre):
        turn = 0.5 * jnp.tanh(0.5 * pre)
        return 0.5 + turn, 0.5 - turn

    tail_pick = lax.broadcasted_iota(jnp.int32, (WRAP, 128), 0) < WRAP // 2

    def expand(row, middle, from_left, from_right):
        tail = jnp.where(
            tail_pick, from_right.astype(jnp.float32), from_left.astype(jnp.float32)
        )
        put(zx, row, jnp.concatenate([middle.astype(jnp.float32), tail], axis=0))

    def split(value, count, n):
        return [value[count * i : count * (i + 1)] for i in range(n)]

    def first_layer(places, product):
        for q, part in zip(places, split(product, width, len(places))):
            pre = part + bias_one
            sigma, rest = parts_of(pre)
            row = 2 * q - 3
            inside = wide[...]
            if row < 0 or row + 1 >= height:
                inside = inside * jnp.where(lane_half, row_ok(row), row_ok(row + 1))
            kept = sigma * inside
            hidden = pre * kept
            slope1[q] = kept + hidden * rest
            put_pair(h1, q, hidden)

    def second_layer(places, product):
        n = len(places)
        rounded, slopes = [], []
        for part in split(product, width, n):
            pre = part + bias_two
            sigma, rest = parts_of(pre)
            hidden = pre * sigma
            slopes.append(sigma + hidden * rest)
            rounded.append(hidden.astype(jnp.bfloat16))
        color = jnp.dot(
            jnp.concatenate(rounded, axis=0), rgb_t[...], preferred_element_type=jnp.float32
        )
        terms = []
        for q, part in zip(places, split(color, width, n)):
            residual = mask_t[q] * (part - target_t[q])
            coarse = residual.astype(jnp.bfloat16)
            fine = (residual - coarse.astype(jnp.float32)).astype(jnp.bfloat16)
            terms.append(jnp.concatenate([coarse, fine], axis=1))
        grad = jnp.dot(
            jnp.concatenate(terms, axis=0), rgb_b[...], preferred_element_type=jnp.float32
        )
        for q, part, slope in zip(places, split(grad, width, n), slopes):
            put_pair(g2, q, part * slope)

    def back_second(places, product):
        for q, part in zip(places, split(product, width, len(places))):
            put_pair(g1, q, part * slope1[q + 1])

    half = height // 2
    stages = (
        (functools.partial(conv, zx, 0, width), first_layer, half + 3, 1 + half),
        (functools.partial(conv, h1, 1, width), second_layer, half + 2, half),
        (functools.partial(conv, g2, 3, width), back_second, half + 1, half - 1),
    )

    results = ((z_ref, latent_out), (m_ref, one_out), (v_ref, two_out), (grad_ref, grad_out))

    def leave(k, q):
        rows = pl.ds(2 * q, 2)
        src, dst = results[k]
        return pltpu.make_async_copy(src.at[rows], dst.at[rows], out_sem.at[k, q])

    for step in range(STEPS):
        last = step == STEPS - 1
        if step > 0:
            for_each(sides, lambda d: halo_arrival(d, step).wait_recv())

        def own_row(r):
            expand(
                r + HALO, stage[step, r], col_in[step, 0, r], col_in[step, 1, r]
            )

        for r in range(height):
            own_row(r)
        tasks = []
        for p, f, _, high in stages[:2]:
            tasks.append((p, f, list(range(2, high - 1))))
            tasks.append((p, f, [high - 1]))
        sweep(tasks)
        p, f, _, high = stages[2]
        sweep([(p, f, list(range(2, high)))])
        for_each(verticals, lambda d: halo_arrival(d, step).wait_recv())

        def halo_row(r):
            expand(r, row_in[step, 0, r], diag_in[step, 0, 0, r], diag_in[step, 0, 1, r])
            expand(
                r + HALO + height,
                row_in[step, 1, r],
                diag_in[step, 1, 0, r],
                diag_in[step, 1, 1, r],
            )

        for r in range(HALO):
            halo_row(r)
        if step == 0:
            loads[5].wait()
            loads[6].wait()

        def update(places, product):
            for q, grads in zip(places, split(product, breadth, len(places))):
                for i in range(2):
                    r = 2 * q + i
                    grad = grads[:, 128 * i : 128 * (i + 1)]
                    if last:
                        grad_ref[r] = grad
                        continue
                    m_ref[r], v_ref[r], z_ref[r] = renew(m_ref[r], v_ref[r], z_ref[r], grad)
                    stage[step + 1, r] = z_ref[r].astype(jnp.bfloat16)
                if last:
                    leave(3, q).start()
                elif step == STEPS - 2:
                    for k in range(3):
                        leave(k, q).start()
            if not last:
                if places[0] == 0:
                    for_each(uppers, lambda d: halo_copy(d, step + 1).start())
                if places[-1] == half - 1:
                    for_each(sides + lowers, lambda d: halo_copy(d, step + 1).start())

        tasks = []
        for p, f, count, high in stages:
            tasks.append((p, f, [0, 1]))
            tasks.append((p, f, list(range(high, count))))
        last_conv = functools.partial(conv, g1, 2, breadth)
        tasks.append((last_conv, update, list(range(half // 2))))
        tasks.append((last_conv, update, list(range(half // 2, half))))
        sweep(tasks)

    for step in range(STEPS):
        for_each(DIRS, lambda d: halo_copy(d, step).wait_send())
    for_each(DIRS, lambda d: aux_copy(d).wait_send())
    for k in range(4):
        for q in range(half):
            leave(k, q).wait()


def body(
    sizes,
    latent,
    moment_one,
    moment_two,
    hole_mask,
    target_rgb,
    kernel_one,
    bias_one,
    kernel_two,
    bias_two,
    rgb_weight,
):
    height, breadth, channels = latent.shape
    width = breadth + WRAP
    rows_n, cols_n, cores_n = sizes
    f32, bf16 = jnp.float32, jnp.bfloat16
    far = pl.BlockSpec(memory_space=pltpu.HBM)
    near = pl.BlockSpec(memory_space=pltpu.VMEM)
    tile = jax.ShapeDtypeStruct(latent.shape, f32)
    half = height // 2
    scratch = [
        *[pltpu.VMEM((height, breadth, channels), f32)] * 4,
        pltpu.VMEM((height, breadth), jnp.int32),
        pltpu.VMEM((4, height, breadth), f32),
        pltpu.VMEM((8, 4, height, breadth), f32),
        pltpu.VMEM((STEPS, height, breadth, channels), bf16),
        pltpu.VMEM((STEPS, 2, HALO, breadth, channels), bf16),
        pltpu.VMEM((STEPS, 2, height, WRAP, channels), bf16),
        pltpu.VMEM((STEPS, 2, 2, HALO, WRAP, channels), bf16),
        pltpu.VMEM((height + 8, width, 3 * channels), bf16),
        pltpu.VMEM((height + 6, width, 3 * channels), bf16),
        pltpu.VMEM((height + 4, width, 3 * channels), bf16),
        pltpu.VMEM((height + 2, width, 3 * channels), bf16),
        pltpu.VMEM((half + 3, width, 2 * channels), f32),
        pltpu.VMEM((4, 12 * channels, 2 * channels), bf16),
        pltpu.VMEM((width, 2 * channels), f32),
        pltpu.VMEM((128, 2 * channels), f32),
        pltpu.VMEM((2 * channels, 128), bf16),
        pltpu.VMEM((256, 2 * channels), bf16),
        pltpu.VMEM((half + 2, 16, breadth + 128), f32),
        pltpu.VMEM((half + 2, width, 128), f32),
        pltpu.VMEM((half + 2, width, 128), f32),
        pltpu.SemaphoreType.DMA((7,)),
        pltpu.SemaphoreType.DMA((4, half)),
        pltpu.SemaphoreType.DMA((STEPS, 8)),
        pltpu.SemaphoreType.DMA((STEPS, 8)),
        pltpu.SemaphoreType.DMA((8,)),
        pltpu.SemaphoreType.DMA((8,)),
    ]
    current, first, second, grad = pl.pallas_call(
        functools.partial(kernel, height, breadth, rows_n, cols_n, cores_n),
        out_shape=(tile, tile, tile, tile),
        in_specs=[far] * 7 + [near] * 3,
        out_specs=(far, far, far, far),
        scratch_shapes=scratch,
        compiler_params=pltpu.CompilerParams(
            collective_id=0, has_side_effects=True, vmem_limit_bytes=60 * 1024 * 1024
        ),
        name="inpaint",
    )(
        latent,
        moment_one,
        moment_two,
        hole_mask,
        target_rgb,
        kernel_one.reshape(9 * channels, channels),
        kernel_two.reshape(9 * channels, channels),
        bias_one.reshape(1, channels),
        bias_two.reshape(1, channels),
        rgb_weight,
    )
    return pl.pallas_call(
        functools.partial(last_update, half),
        out_shape=(tile, tile, tile),
        in_specs=[far] * 4,
        out_specs=(far, far, far),
        scratch_shapes=[
            *[pltpu.VMEM((height, breadth, channels), f32)] * 4,
            pltpu.SemaphoreType.DMA((4, half)),
            pltpu.SemaphoreType.DMA((3, half)),
        ],
        compiler_params=pltpu.CompilerParams(vmem_limit_bytes=60 * 1024 * 1024),
        name="last_update",
    )(current, first, second, grad)


def solution(mesh):
    sizes = (mesh.shape["row"], mesh.shape["col"], mesh.shape["cores"])
    tile = P(("parts", "row", "cores"), "col", None)
    return jax.shard_map(
        functools.partial(body, sizes),
        mesh=mesh,
        in_specs=(
            tile,
            tile,
            tile,
            P(("parts", "row", "cores"), "col"),
            P(None, ("parts", "row", "cores"), "col"),
            P(),
            P(),
            P(),
            P(),
            P(),
        ),
        out_specs=(tile, tile, tile),
        check_vma=False,
    )
```
